32 devices in a mesh: dp: 8 (over z, y), seq: 4 (over x, core).
Axes of the slice: x: 2, y: 2, z: 4, core: 2. Of those that a mesh axis runs over, the one named last changes fastest.
Arguments:
- activations: bfloat16 [4096, 1536], P(('dp', 'seq')), may hold values from -6 to 6
- cotangent: bfloat16 [4096, 1536], P(('dp', 'seq')), may hold values from -6 to 6
- doc_lengths: int32 [1, 8], replicated, may hold values from 1 to 2048, as said below
- routes: int32 [4096, 4], P(('dp', 'seq')), may hold values from 0 to 7, all different within a row; in each aligned block of 128 rows (0 to 127, 128 to 255, ...) at most 128 rows name the same one
- norm_gains: bfloat16 [2, 2, 1536], P(None, None, ('dp', 'seq')), may hold values from 0.5 to 1.5
- w_qkv: bfloat16 [2, 1536, 2048], P(None, ('dp', 'seq')), may hold values from -0.15625 to 0.15625
- w_out: bfloat16 [2, 1536, 1536], P(None, None, ('dp', 'seq')), may hold values from -0.875 to 0.875
- w_router: bfloat16 [2, 1536, 8], P(None, ('dp', 'seq')), may hold values from -0.078125 to 0.078125
- w_gate_up: bfloat16 [2, 8, 1536, 1536], P(None, 'dp'), may hold values from -0.15625 to 0.15625
- w_down: bfloat16 [2, 8, 768, 1536], P(None, 'dp'), may hold values from -0.4375 to 0.4375
Outputs:
- layer_out: bfloat16 [4096, 1536], P(('dp', 'seq'))
- input_grad: float32 [4096, 1536], P(('dp', 'seq'))
- gain_grad: float32 [2, 2, 1536], P(None, None, ('dp', 'seq'))
- qkv_grad: float32 [2, 1536, 2048], P(None, ('dp', 'seq'))
- out_proj_grad: float32 [2, 1536, 1536], P(None, None, ('dp', 'seq'))
- router_grad: float32 [2, 1536, 8], P(None, ('dp', 'seq'))
- gate_up_grad: float32 [2, 8, 1536, 1536], P(None, 'dp', 'seq')
- down_grad: float32 [2, 8, 768, 1536], P(None, 'dp', 'seq')
The draws below stay inside these ranges and needn't reach their ends.
Inputs may be any that keep to these rules, and one draw needn't show every extreme that they name: `doc_lengths`: each row lists 8 - 1 documents and then the padded tail, sums to 4096, and one of its documents has exactly 2048 tokens. `routes`: A token names 4 different experts; in the rows of one device no expert is named more than 128 times.
All inputs are finite; a program needn't handle non-finite values.
Results may differ from the reference program's by a relative error of at most 0.025.
Values may be sent and summed in bfloat16 or wider, within the bound.
No kernel may reach another device: no remote copies, remote signals or barrier semaphores. Data moves between devices by JAX's collectives and lax.ppermute only.
A program may use at most 256 MiB of HBM per device.

```python
import math
import jax
import jax.numpy as jnp
import numpy as np
from jax import lax

D = 1536
HEADS = 12
KV_HEADS = 2
HEAD = 128
FF = 768
TOP = 4
WINDOW = 1024
DOCS = 8
LAYERS = 2
TOK_DEV = 128
EXPERTS = 8
TOKENS = 4096
LENGTH = 4096
SEQS = 1
CAP = 128
QKV = 2048


def draw_doc_lengths(key, part):
    key = jax.random.fold_in(key, 11)
    pad_most = LENGTH // 16
    big_doc = LENGTH // 2
    spread = big_doc - pad_most

    def per_sequence(seq_key):
        key_pad, key_cut, key_order = jax.random.split(seq_key, 3)
        pad_length = jax.random.randint(key_pad, (), 1, pad_most + 1).astype(jnp.int32)
        cut_points = jnp.sort(jax.random.permutation(key_cut, spread - 1)[:DOCS - 3] + 1).astype(jnp.int32)
        bounds = jnp.concatenate([jnp.zeros((1,), jnp.int32), cut_points, jnp.full((1,), spread, jnp.int32)])
        pieces = bounds[1:] - bounds[:-1]
        pieces = pieces.at[-1].add(pad_most - pad_length)
        doc_sizes = jax.random.permutation(key_order, jnp.concatenate([jnp.full((1,), big_doc, jnp.int32), pieces]))
        return jnp.concatenate([doc_sizes, pad_length[None]]).astype(jnp.int32)
    return jax.vmap(per_sequence)(jax.random.split(key, SEQS))


def spiked(drawn, stream_key, source, target, parts, factor):
    owner, partner = [(jnp.arange(drawn.shape[dim]) // (drawn.shape[dim] // parts)).reshape([-1 if axis == dim else 1 for axis in range(drawn.ndim)]) for dim in (source, target)]
    chosen = jax.random.permutation(stream_key, parts)[partner]
    strong = (owner == chosen) | (owner == (partner + parts // 2) % parts)
    return jnp.where(strong, factor * drawn, drawn)


def shard_levels(stream_key, extent, cuts, low, high):
    level = 1.0
    for dim, parts in cuts:
        heights = jax.random.uniform(jax.random.fold_in(jax.random.fold_in(stream_key, 6), dim), (parts,), jnp.float32, low / len(cuts), high / len(cuts))
        level = level * jnp.repeat(jnp.exp(heights), extent[dim] // parts).reshape((-1,) + (1,) * (len(extent) - 1 - dim))
    return level


def routed_block(key, own, number, rows, number_of, top, limit, skew):
    order = jax.random.permutation(key, number_of)
    heavy_load, usual = shares(number_of, rows * top, limit, skew, True), shares(number_of, rows * top, limit, skew, False)
    places = jnp.arange(number_of)

    def named(sizes, turn):
        used = int((sizes > 0).sum())
        fixed = max(1, used // 4)
        passed = fixed + (places - fixed + turn * (used - fixed)) % max(1, number_of - fixed)
        return jnp.zeros((number_of,), jnp.int32).at[order[jnp.where(places < fixed, places, passed)]].set(jnp.asarray(sizes, jnp.int32))

    sizes = jnp.where(number % 4 == 0, named(heavy_load, number // 4), named(usual, number - number // 4 - 1))
    mixed = jax.random.permutation(jax.random.fold_in(own, 3), number_of)
    giver, taker = mixed[0:number_of // 2 * 2:2], mixed[1:number_of // 2 * 2:2]
    slack = jnp.minimum(sizes[giver] - 1, limit - sizes[taker]) // 2
    slack = jnp.where((giver == order[0]) | (taker == order[0]) | (sizes[taker] == 0), 0, jnp.maximum(slack, 0))
    passed = jax.random.randint(jax.random.fold_in(own, 4), (number_of // 2,), 0, 1 << 20) % (slack + 1)
    sizes = sizes.at[giver].add(-passed).at[taker].add(passed)
    members = jnp.searchsorted(jnp.cumsum(sizes), jnp.arange(rows * top), side="right").astype(jnp.int32)
    table = members.reshape(top, rows).T
    table = table[jax.random.permutation(jax.random.fold_in(own, 1), rows)]
    turn = jax.random.randint(jax.random.fold_in(own, 2), (rows, 1), 0, top)
    return jnp.take_along_axis(table, (jnp.arange(top)[None, :] + turn) % top, axis=1)


def shares(number_of, total, reach, lean, full):
    loads = [(1 << 20) // math.isqrt(rank ** lean) + 1 for rank in range(1, number_of + 1)]
    largest = reach if full else min(reach, max(-(-total // number_of), total * loads[0] // sum(loads)))
    least = 1 if total - largest >= number_of - 1 else 0
    given, surplus = [largest] + [least] * (number_of - 1), total - largest - least * (number_of - 1)
    while surplus > 0:
        free = [i for i in range(1, number_of) if given[i] < largest] or [i for i in range(1, number_of) if given[i] < reach]
        pool, left = sum([loads[i] for i in free]), surplus
        for i in free:
            addition = min(reach - given[i], max(1, left * loads[i] // pool), surplus)
            given[i] = given[i] + addition
            surplus = surplus - addition
    return np.array(given)


def gaussian(rng, shape, scale, limit, cuts=(), kind=jnp.bfloat16):
    values = scale * jax.random.normal(rng, shape, jnp.float32)
    if cuts:
        values = values * shard_levels(rng, shape, cuts, -0.22, 0.18)
    return jnp.clip(values, -limit, limit).astype(kind)


def noise_with(key, extent, deviation, limit, cuts, heavy, kind=jnp.bfloat16):
    values = deviation * jax.random.normal(key, extent, jnp.float32)
    if cuts:
        values = values * shard_levels(key, extent, cuts, -0.22, 0.18)
    return jnp.clip(spiked(values, jax.random.fold_in(key, 3), *heavy), -limit, limit).astype(kind)


def setup_inputs(seed: int = 0) -> dict:
    streams_of = jax.random.split(jax.random.key(seed), 11)
    activations = gaussian(streams_of[0], (TOKENS, D), 1.0, 6.0, ((0, 32),))
    cotangent = noise_with(streams_of[1], (TOKENS, D), 1.0, 6.0, ((0, 32),), (0, 1, 32, 2.75))
    doc_lengths = draw_doc_lengths(jax.random.fold_in(streams_of[10], 71), 0)
    routes_keys = jax.random.split(jax.random.fold_in(streams_of[3], 1), TOKENS // TOK_DEV)
    routes_turns = jax.random.permutation(jax.random.fold_in(streams_of[3], 3), TOKENS // TOK_DEV)
    routes = jax.vmap(lambda own, number: routed_block(jax.random.fold_in(streams_of[3], 2), own, number, TOK_DEV, EXPERTS, TOP, CAP, 1))(routes_keys, routes_turns).reshape((TOKENS, TOP))
    norm_gains = jnp.clip(1.0 + 0.1 * jax.random.normal(streams_of[4], (LAYERS, 2, D), jnp.float32), 0.5, 1.5).astype(jnp.bfloat16)
    w_qkv = gaussian(streams_of[5], (LAYERS, D, QKV), D ** -0.5, 0.15625, ((1, 32),))
    w_out = gaussian(streams_of[6], (LAYERS, HEADS * HEAD, D), (HEADS * HEAD // 32) ** -0.5, 0.875, ((2, 32),))
    w_router = gaussian(streams_of[7], (LAYERS, D, EXPERTS), (4 * D) ** -0.5, 0.078125, ((1, 32),))
    w_gate_up = gaussian(streams_of[8], (LAYERS, EXPERTS, D, 2 * FF), D ** -0.5, 0.15625, ((1, 8),))
    w_down = gaussian(streams_of[9], (LAYERS, EXPERTS, FF, D), (FF // 4) ** -0.5, 0.4375, ((1, 8),))
    return {"activations": activations, "cotangent": cotangent, "doc_lengths": doc_lengths, "routes": routes, "norm_gains": norm_gains, "w_qkv": w_qkv, "w_out": w_out, "w_router": w_router, "w_gate_up": w_gate_up, "w_down": w_down}


norm_eps = 1e-06
rope_base = 1000000.0
highest = lax.Precision.HIGHEST
tile_rows = 128

@jax.custom_vjp
def low(v):
    return lax.optimization_barrier(v.astype(jnp.bfloat16)).astype(jnp.float32)

@jax.custom_vjp
def low_back(v):
    return v

def low_keep(v):
    return (low(v), None)

def low_pass(kept, grad):
    return (grad,)

def back_keep(v):
    return (v, None)

def back_low(kept, grad):
    return (low(grad),)
low.defvjp(low_keep, low_pass)
low_back.defvjp(back_keep, back_low)

def doc_labels(token_index, doc_lengths, seq_length):
    doc_total = doc_lengths.shape[1]
    doc_ends = jnp.cumsum(doc_lengths, axis=1).astype(jnp.int32)
    clamped = jnp.maximum(token_index, 0)
    seq_number = (clamped // seq_length).astype(jnp.int32)
    position = (clamped % seq_length).astype(jnp.int32)
    seq_pick = seq_number[:, None] == jnp.arange(doc_lengths.shape[0], dtype=jnp.int32)[None, :]
    token_ends = lax.optimization_barrier(jnp.sum(jnp.where(seq_pick[:, :, None], doc_ends[None, :, :], 0), axis=1)).astype(jnp.int32)
    doc_number = lax.optimization_barrier(jnp.sum((position[:, None] >= token_ends).astype(jnp.int32), axis=1)).astype(jnp.int32)
    doc_label = jnp.where(token_index >= 0, seq_number * doc_total + doc_number, -1).astype(jnp.int32)
    is_valid = (doc_number < doc_total - 1).astype(jnp.float32)
    return (doc_label, is_valid, position)

def rope_turn(vectors, position, direction):
    half_width = vectors.shape[-1] // 2
    frequency = rope_base ** (-jnp.arange(half_width, dtype=jnp.float32) * 2.0 / vectors.shape[-1])
    angles = position.astype(jnp.float32)[:, None] * frequency[None, :]
    cosine = jnp.cos(angles)[:, None, :]
    sine_part = direction * jnp.sin(angles)[:, None, :]
    first_half = vectors[..., :half_width]
    second_half = vectors[..., half_width:]
    return jnp.concatenate([first_half * cosine - second_half * sine_part, second_half * cosine + first_half * sine_part], axis=-1)

def norm_rows(stream, gain):
    return stream * lax.rsqrt(lax.optimization_barrier(jnp.mean(stream * stream, axis=-1, keepdims=True)) + norm_eps) * gain

def attention(queries, key_vecs, value_vecs, labels):
    total_rows = queries.shape[0]
    block_rows = math.gcd(512, total_rows)
    kv_count = key_vecs.shape[1]
    share_count = queries.shape[1] // kv_count
    score_scale = queries.shape[-1] ** (-0.5)
    pad_keys = jnp.concatenate([jnp.zeros((WINDOW,) + key_vecs.shape[1:], jnp.float32), key_vecs])
    pad_values = jnp.concatenate([jnp.zeros((WINDOW,) + value_vecs.shape[1:], jnp.float32), value_vecs])
    pad_labels = jnp.concatenate([jnp.full((WINDOW,), -1, jnp.int32), labels])

    def one_block(block_start):
        query_piece = lax.dynamic_slice_in_dim(queries, block_start, block_rows, 0).reshape(block_rows, kv_count, share_count, -1)
        key_piece = lax.dynamic_slice_in_dim(pad_keys, block_start, block_rows + WINDOW, 0)
        value_piece = lax.dynamic_slice_in_dim(pad_values, block_start, block_rows + WINDOW, 0)
        query_labels = lax.dynamic_slice_in_dim(labels, block_start, block_rows, 0)
        key_labels = lax.dynamic_slice_in_dim(pad_labels, block_start, block_rows + WINDOW, 0)
        query_pos = block_start + jnp.arange(block_rows, dtype=jnp.int32)
        key_pos = block_start - WINDOW + jnp.arange(block_rows + WINDOW, dtype=jnp.int32)
        distance = query_pos[:, None] - key_pos[None, :]
        keep_mask = (query_labels[:, None] == key_labels[None, :]) & (distance >= 0) & (distance < WINDOW)
        scores = low_back(jnp.einsum('qhgd,khd->hgqk', query_piece, key_piece, precision=highest) * score_scale)
        prob_rows = low(jax.nn.softmax(jnp.where(keep_mask[None, None], scores, -jnp.inf), axis=-1))
        block_out = jnp.einsum('hgqk,khd->qhgd', prob_rows, value_piece, precision=highest)
        return block_out.reshape(block_rows, -1)
    starts = jnp.arange(total_rows // block_rows, dtype=jnp.int32) * block_rows
    return lax.map(jax.checkpoint(one_block), starts).reshape(total_rows, -1)

def expert_mix(normed, w_gate_up, w_down, routes, gates):
    total_rows, model_width = normed.shape
    top_count = routes.shape[1]
    expert_count = w_gate_up.shape[0]
    ff_width = w_down.shape[1]
    assign_count = total_rows * top_count
    flat_expert = routes.reshape(assign_count).astype(jnp.int32)
    chosen_mask = flat_expert[:, None] == jnp.arange(expert_count, dtype=jnp.int32)[None, :]
    counts = lax.optimization_barrier(jnp.sum(chosen_mask.astype(jnp.int32), axis=0)).astype(jnp.int32)
    padded = (counts + tile_rows - 1) // tile_rows * tile_rows
    padded_start = (jnp.cumsum(padded) - padded).astype(jnp.int32)
    plain_start = (jnp.cumsum(counts) - counts).astype(jnp.int32)
    order = jnp.argsort(flat_expert, stable=True).astype(jnp.int32)
    sorted_expert = flat_expert[order]
    dest_sorted = (padded_start[sorted_expert] + jnp.arange(assign_count, dtype=jnp.int32) - plain_start[sorted_expert]).astype(jnp.int32)
    destination = jnp.zeros((assign_count,), jnp.int32).at[order].set(dest_sorted)
    tile_count = (assign_count + expert_count * (tile_rows - 1)) // tile_rows + 1
    source = jnp.full((tile_count * tile_rows,), assign_count, jnp.int32).at[destination].set(jnp.arange(assign_count, dtype=jnp.int32))
    tile_first = jnp.arange(tile_count, dtype=jnp.int32) * tile_rows
    tile_expert = jnp.minimum(lax.optimization_barrier(jnp.sum((tile_first[:, None] >= (padded_start + padded)[None, :]).astype(jnp.int32), axis=1)), expert_count - 1).astype(jnp.int32)
    token_rows = jnp.concatenate([normed, jnp.zeros((1, model_width), jnp.float32)])
    gathered = low_back(token_rows[jnp.where(source < assign_count, source // top_count, total_rows)])

    def one_tile(packed):
        tile_input, expert_index = packed
        up_gate = low_back(jnp.dot(tile_input, w_gate_up[expert_index], precision=highest))
        hidden = low(jax.nn.silu(up_gate[:, :ff_width]) * up_gate[:, ff_width:])
        return low_back(low(jnp.dot(hidden, w_down[expert_index], precision=highest)))
    outputs = lax.map(jax.checkpoint(one_tile), (gathered.reshape(tile_count, tile_rows, model_width), tile_expert))
    outputs = outputs.reshape(tile_count * tile_rows, model_width)
    picked = outputs[destination].reshape(total_rows, top_count, model_width)
    return lax.optimization_barrier(jnp.sum(gates[:, :, None] * picked, axis=1))

def one_layer(stream, gains, w_qkv, w_out, w_router, w_gate_up, w_down, labels, valid, position, routes):
    total_rows = stream.shape[0]
    q_width = HEADS * HEAD
    kv_width = KV_HEADS * HEAD
    normed_one = low(norm_rows(stream, gains[0]))
    mixed_rows = jnp.dot(normed_one, w_qkv, precision=highest)
    queries = low(rope_turn(low_back(mixed_rows[:, :q_width]).reshape(total_rows, HEADS, HEAD), position, 1.0))
    key_vecs = low(rope_turn(low_back(mixed_rows[:, q_width:q_width + kv_width]).reshape(total_rows, KV_HEADS, HEAD), position, 1.0))
    value_vecs = low(low_back(mixed_rows[:, q_width + kv_width:])).reshape(total_rows, KV_HEADS, HEAD)
    attended = attention(queries, key_vecs, value_vecs, labels) * valid[:, None]
    attended = low_back(low(attended))
    stream_mid = stream + low_back(jnp.dot(attended, w_out, precision=highest))
    normed_two = low(norm_rows(stream_mid, gains[1]))
    logits = low_back(jnp.dot(normed_two, w_router, precision=highest))
    chosen = jnp.take_along_axis(logits, routes, axis=1)
    gate_probs = jax.nn.softmax(chosen, axis=1)
    return stream_mid + expert_mix(normed_two, w_gate_up, w_down, routes, gate_probs)

def reference(activations, cotangent, doc_lengths, routes, norm_gains, w_qkv, w_out, w_router, w_gate_up, w_down):
    total_rows = activations.shape[0]
    token_index = jnp.arange(total_rows, dtype=jnp.int32)
    labels, valid, position = doc_labels(token_index, doc_lengths, LENGTH)

    def forward(stream, gains, qkv_all, out_all, router_all, gate_up_all, down_all):
        for layer_index in range(gains.shape[0]):
            stream = one_layer(stream, gains[layer_index], qkv_all[layer_index], out_all[layer_index], router_all[layer_index], gate_up_all[layer_index], down_all[layer_index], labels, valid, position, routes)
        return stream
    result, pullback = jax.vjp(forward, activations.astype(jnp.float32), norm_gains.astype(jnp.float32), w_qkv.astype(jnp.float32), w_out.astype(jnp.float32), w_router.astype(jnp.float32), w_gate_up.astype(jnp.float32), w_down.astype(jnp.float32))
    grads = pullback(cotangent.astype(jnp.float32))
    return (result.astype(jnp.bfloat16), grads[0], grads[1], grads[2], grads[3], grads[4], grads[5], grads[6])
```

```python
import jax
import jax.numpy as jnp
from jax import lax
from jax.sharding import PartitionSpec as P

HEADS = 12
KV_HEADS = 2
HEAD = 128
WINDOW = 1024
SEQ_LEN = 8192


norm_eps = 1e-06
rope_base = 1000000.0


ALL = ("dp", "seq")
CORES = 2
LINE_MOST = 4
f32 = jnp.float32
bf16 = jnp.bfloat16


def dot(left, right, dims):
    return lax.dot_general(left, right, (dims, ((), ())), preferred_element_type=f32)


class Wires:
    def __init__(self):
        self.dp_count = lax.axis_size("dp")
        self.seq_count = lax.axis_size("seq")
        self.pairs = self.seq_count // CORES
        self.length = self.dp_count // 2
        dp_index = lax.axis_index("dp")
        seq_index = lax.axis_index("seq")
        self.dp_index = dp_index
        self.line = dp_index // 2
        self.side = dp_index % 2
        self.pair = seq_index // CORES
        self.core = seq_index % CORES
        self.chip = dp_index * self.pairs + self.pair
        self.chips = self.dp_count * self.pairs
        self.by_line = self.length <= LINE_MOST and self.pairs == 2

    def to_core(self, value):
        return lax.ppermute(value, "seq", [(i, i ^ 1) for i in range(self.seq_count)])

    def to_pair(self, value):
        return lax.ppermute(value, "seq", [(i, i ^ 2) for i in range(self.seq_count)])

    def to_side(self, value):
        return lax.ppermute(value, "dp", [(i, i ^ 1) for i in range(self.dp_count)])

    def up(self, value, first, last):
        return lax.ppermute(
            value, "dp", [(i, i + 2) for i in range(2 * first, 2 * min(last, self.length - 1))]
        )

    def down(self, value, first, last):
        return lax.ppermute(
            value, "dp", [(i, i - 2) for i in range(2 * max(first, 1), 2 * last)]
        )

    def chips_on(self, value, steps):
        count = self.dp_count * self.seq_count
        offset = steps * CORES
        first, last = (max(0, -offset), min(count, count - offset))
        return lax.ppermute(value, ALL, [(i, i + offset) for i in range(first, last)])

    def ordered(self, flag, own, other, axis):
        return jnp.stack(
            [jnp.where(flag == 0, own, other), jnp.where(flag == 0, other, own)], axis=axis
        )

    def line_gather(self, value):
        count = self.length
        ups, downs = [value], [value]
        for step in range(1, count):
            ups.append(self.up(ups[-1], step - 1, count))
            downs.append(self.down(downs[-1], 0, count - step + 1))
        return [value] + [
            jnp.where(self.line >= k, ups[k], downs[count - k]) for k in range(1, count)
        ]

    def line_scatter(self, blocks):
        count = self.length
        total = blocks[0].astype(f32)
        for rising in (True, False):
            carried = None
            for step in range(1, count):
                piece = blocks[step] if rising else blocks[count - step]
                if carried is not None:
                    piece = (piece.astype(f32) + carried.astype(f32)).astype(bf16)
                if rising:
                    carried = self.up(piece, 0, step)
                else:
                    carried = self.down(piece, count - step, count)
            if carried is not None:
                total = total + carried.astype(f32)
        return total

    def token_gather(self, value):
        if not self.by_line:
            return [lax.all_gather(value, "dp", axis=0, tiled=True)]
        return [
            jnp.concatenate([block, self.to_side(block)], axis=0)
            for block in self.line_gather(value)
        ]

    def token_scatter(self, blocks):
        if not self.by_line:
            return lax.psum_scatter(blocks[0], "dp", scatter_dimension=0, tiled=True).astype(f32)
        rows = blocks[0].shape[0] // 2
        summed = []
        for k, block in enumerate(blocks):
            total = block[:rows].astype(f32) + self.to_side(block[rows:]).astype(f32)
            summed.append(total if k == 0 else total.astype(bf16))
        return self.line_scatter(summed)

    def token_owner(self):
        if not self.by_line:
            return [list(range(self.dp_count))]
        owners = []
        for k in range(self.length):
            place = lax.rem(self.line - k + self.length, self.length)
            owners.append([place * 2 + self.side, place * 2 + 1 - self.side])
        return owners

    def core_groups(self):
        count = self.dp_count * self.seq_count
        return [list(range(core, count, CORES)) for core in range(CORES)]

    def chip_gather(self, block):
        rows, columns = block.shape
        if not self.by_line:
            return lax.all_gather(
                block, ALL, axis=0, tiled=True, axis_index_groups=self.core_groups()
            )
        half = rows // 2
        whole = jnp.zeros((self.chips * rows, columns), block.dtype)
        for k, piece in enumerate(self.line_gather(block)):
            one, two = piece[:half], piece[half:]
            one = self.ordered(self.side, one, self.to_side(one), 0)
            two = self.ordered(self.pair, two, self.to_pair(two), 0)
            one = self.ordered(self.pair, one, self.to_pair(one), 1)
            two = self.ordered(self.side, two, self.to_side(two), 0)
            piece = jnp.stack([one, two], axis=2).reshape(4 * rows, columns)
            place = lax.rem(self.line - k + self.length, self.length)
            whole = lax.dynamic_update_slice(whole, piece, (place * 4 * rows, 0))
        return whole

    def picked(self, flag, stacked, axis):
        first, second = (
            lax.index_in_dim(stacked, 0, axis, keepdims=False),
            lax.index_in_dim(stacked, 1, axis, keepdims=False),
        )
        return jnp.where(flag == 0, first, second), jnp.where(flag == 0, second, first)

    def chip_scatter(self, whole):
        columns = whole.shape[1]
        rows = whole.shape[0] // self.chips
        if not self.by_line:
            return lax.psum_scatter(
                whole,
                ALL,
                scatter_dimension=0,
                tiled=True,
                axis_index_groups=self.core_groups(),
            ).astype(f32)
        half = rows // 2
        summed = []

        def step(flag, stacked, axis, move):
            kept, sent = self.picked(flag, stacked, axis)
            return (kept.astype(f32) + move(sent).astype(f32)).astype(bf16)

        for k in range(self.length):
            place = lax.rem(self.line - k + self.length, self.length)
            piece = lax.dynamic_slice(whole, (place * 4 * rows, 0), (4 * rows, columns))
            piece = piece.reshape(2, 2, 2, half, columns)
            one, two = piece[:, :, 0], piece[:, :, 1]
            one = step(self.pair, one, 1, self.to_pair)
            two = step(self.side, two, 0, self.to_side)
            one = step(self.side, one, 0, self.to_side)
            two = step(self.pair, two, 0, self.to_pair)
            summed.append(jnp.concatenate([one, two], axis=0))
        return self.line_scatter(summed)

    def chip_rows(self, value):
        return jnp.concatenate([value, self.to_core(value)], axis=0)

    def chip_sum(self, value):
        rows = value.shape[0] // 2
        return value[:rows] + self.to_core(value[rows:].astype(bf16)).astype(f32)

    def seq_scatter(self, value):
        rows, columns = value.shape
        if self.pairs != 2:
            return lax.psum_scatter(value, "seq", scatter_dimension=0, tiled=True).astype(f32)
        piece = value.reshape(2, 2, rows // 4, columns)
        kept, sent = self.picked(self.core, piece, 1)
        piece = (kept.astype(f32) + self.to_core(sent).astype(f32)).astype(bf16)
        kept, sent = self.picked(self.pair, piece, 0)
        return kept.astype(f32) + self.to_pair(sent).astype(f32)


def doc_labels(token_index, doc_lengths, seq_length):
    doc_total = doc_lengths.shape[1]
    doc_ends = jnp.cumsum(doc_lengths, axis=1)
    clamped = jnp.maximum(token_index, 0)
    seq_number = clamped // seq_length
    position = clamped % seq_length
    seq_pick = seq_number[:, None] == jnp.arange(doc_lengths.shape[0], dtype=jnp.int32)[None, :]
    token_ends = jnp.sum(jnp.where(seq_pick[:, :, None], doc_ends[None, :, :], 0), axis=1)
    doc_number = jnp.sum((position[:, None] >= token_ends).astype(jnp.int32), axis=1)
    doc_label = jnp.where(token_index >= 0, seq_number * doc_total + doc_number, -1)
    is_valid = (doc_number < doc_total - 1).astype(jnp.float32)
    return (doc_label, is_valid, position)


def rope_turn(vectors, position, direction):
    half_width = vectors.shape[-1] // 2
    frequency = rope_base ** (-jnp.arange(half_width, dtype=jnp.float32) * 2.0 / vectors.shape[-1])
    angles = position.astype(jnp.float32)[:, None] * frequency[None, :]
    cosine = jnp.cos(angles)[:, None, :]
    sine_part = direction * jnp.sin(angles)[:, None, :]
    first_half = vectors[..., :half_width]
    second_half = vectors[..., half_width:]
    return jnp.concatenate(
        [
            first_half * cosine - second_half * sine_part,
            second_half * cosine + first_half * sine_part,
        ],
        axis=-1,
    )


def norm_scale(stream):
    return lax.rsqrt(jnp.mean(stream * stream, axis=-1, keepdims=True) + norm_eps)


def norm_back(stream, scale, gain, out_grad):
    gain_grad = jnp.sum(out_grad * stream * scale, axis=0)
    scaled_grad = out_grad * gain
    stream_grad = scale * scaled_grad - stream * scale**3 * jnp.mean(
        scaled_grad * stream, axis=-1, keepdims=True
    )
    return (gain_grad, stream_grad)


def keep_rule(query_index, key_index, query_label, key_label):
    distance = query_index[:, None] - key_index[None, :]
    same_doc = query_label[:, None] == key_label[None, :]
    return same_doc & (distance >= 0) & (distance < WINDOW)


def attend_forward(queries, keys, values, keep_mask):
    scores = jnp.einsum("qhd,kd->hqk", queries, keys, preferred_element_type=f32) * HEAD ** (-0.5)
    scores = jnp.where(keep_mask[None], scores, -jnp.inf)
    row_top = jnp.max(scores, axis=-1, keepdims=True)
    weights = jnp.exp(scores - row_top)
    row_total = jnp.sum(weights, axis=-1, keepdims=True)
    prob_rows = (weights / row_total).astype(bf16)
    out = jnp.einsum("hqk,kd->qhd", prob_rows, values, preferred_element_type=f32)
    return (out, row_top + jnp.log(row_total))


def attend_backward(queries, keys, values, head_grad, log_total, keep_mask):
    score_scale = HEAD ** (-0.5)
    scores = jnp.einsum("qhd,kd->hqk", queries, keys, preferred_element_type=f32) * score_scale
    prob_rows = jnp.where(keep_mask[None], jnp.exp(scores - log_total), 0.0)
    prob_grad = jnp.einsum("qhd,kd->hqk", head_grad, values, preferred_element_type=f32)
    row_dot = jnp.sum(prob_rows * prob_grad, axis=-1, keepdims=True)
    score_grad = (prob_rows * (prob_grad - row_dot)).astype(bf16)
    query_grad = (
        jnp.einsum("hqk,kd->qhd", score_grad, keys, preferred_element_type=f32) * score_scale
    )
    key_grad = (
        jnp.einsum("hqk,qhd->kd", score_grad, queries, preferred_element_type=f32) * score_scale
    )
    value_grad = jnp.einsum(
        "hqk,qhd->kd", prob_rows.astype(bf16), head_grad, preferred_element_type=f32
    )
    return (query_grad, key_grad, value_grad)


def expert_gates(normed, router, routes, expert_ids):
    logits = dot(normed, router, ((1,), (0,)))
    named = jnp.any(routes[:, :, None] == expert_ids[None, None, :], axis=1)
    top = jnp.max(jnp.where(named, logits, -jnp.inf), axis=1, keepdims=True)
    weights = jnp.where(named, jnp.exp(logits - top), 0.0)
    return weights / jnp.sum(weights, axis=1, keepdims=True), named


def per_device(
    activations,
    cotangent,
    doc_lengths,
    routes,
    norm_gains,
    w_qkv,
    w_out,
    w_router,
    w_gate_up,
    w_down,
):
    wires = Wires()
    tok_rows, model_width = activations.shape
    layer_count = w_qkv.shape[0]
    heads_here = HEADS // CORES
    q_width = heads_here * HEAD
    qkv_width = q_width + 2 * HEAD
    ff_width = w_down.shape[2]
    expert_count = w_router.shape[2]
    chip_tokens = CORES * tok_rows
    device_count = wires.dp_count * wires.seq_count
    seq_length = min(SEQ_LEN, tok_rows * device_count)
    depth = min(-(-(WINDOW - 1) // chip_tokens), wires.chips - 1)
    core = wires.core

    def chip_index_of(first_chip, chips):
        block = first_chip + jnp.arange(chips, dtype=jnp.int32)
        order = jnp.stack([core, 1 - core]).astype(jnp.int32)
        start = block[:, None] * chip_tokens + order[None, :] * tok_rows
        return (start[:, :, None] + jnp.arange(tok_rows, dtype=jnp.int32)).reshape(-1)

    query_index = chip_index_of(wires.chip, 1)
    key_index = chip_index_of(wires.chip - depth, depth + 1)
    query_label, query_valid, position = doc_labels(query_index, doc_lengths, seq_length)
    key_label = doc_labels(key_index, doc_lengths, seq_length)[0]
    keep_mask = keep_rule(query_index, key_index, query_label, key_label)
    expert_ids = jnp.arange(expert_count, dtype=jnp.int32)
    my_expert = (expert_ids == wires.dp_index)[None, :]
    all_routes = lax.all_gather(routes, "dp", axis=0)
    block_routes = [
        jnp.concatenate(
            [lax.dynamic_index_in_dim(all_routes, owner, 0, keepdims=False) for owner in owners]
        )
        for owners in wires.token_owner()
    ]

    small_width = -(-(expert_count + 2) // 128) * 128

    def packed_weights(layer_index):
        out_rows = w_out[layer_index].T
        qkv = w_qkv[layer_index]
        small = jnp.concatenate([w_router[layer_index], norm_gains[layer_index].T], axis=1)
        small = jnp.pad(small, ((0, 0), (0, small_width - small.shape[1])))
        fronts, backs = [], []
        for c in range(CORES):
            fronts.append(
                jnp.concatenate(
                    [
                        qkv[:, c * q_width : (c + 1) * q_width],
                        qkv[:, HEADS * HEAD + c * HEAD :][:, :HEAD],
                        qkv[:, (HEADS + KV_HEADS + c) * HEAD :][:, :HEAD],
                        small,
                    ],
                    axis=1,
                )
            )
            backs.append(out_rows[:, c * q_width : (c + 1) * q_width])
        result = []
        for first, second in (fronts, backs):
            kept = jnp.where(core == 0, first, second)
            sent = jnp.where(core == 0, second, first)
            block = wires.ordered(core, kept, wires.to_core(sent), 0)
            result.append(block.reshape(2 * kept.shape[0], kept.shape[1]))
        return result

    held_weights = []
    for layer_index in range(layer_count):
        front, back = packed_weights(layer_index)
        front = wires.chip_gather(front)
        back = wires.chip_gather(back)
        small = front[:, qkv_width:]
        held_weights.append(
            (
                small[:, expert_count : expert_count + 2].astype(f32).T,
                front[:, :qkv_width],
                back,
                small[:, :expert_count],
            )
        )
    stream = activations.astype(f32)
    stored = []
    for layer_index in range(layer_count):
        gain_rows, qkv_here, out_here, router = held_weights[layer_index]
        gate_up_here = w_gate_up[layer_index, 0]
        down_here = w_down[layer_index, 0]
        scale_one = norm_scale(stream)
        normed_one = wires.chip_rows((stream * scale_one * gain_rows[0]).astype(bf16))
        mixed = dot(normed_one, qkv_here, ((1,), (0,)))
        queries = rope_turn(
            mixed[:, :q_width].reshape(chip_tokens, heads_here, HEAD), position, 1.0
        ).astype(bf16)
        own_keys = rope_turn(mixed[:, None, q_width : q_width + HEAD], position, 1.0)[:, 0]
        own_pair = jnp.concatenate([own_keys, mixed[:, q_width + HEAD :]], axis=1).astype(bf16)
        table = jnp.concatenate(
            [wires.chips_on(own_pair, step) for step in range(depth, 0, -1)] + [own_pair], axis=0
        )
        keys, values = table[:, :HEAD], table[:, HEAD:]
        attended, log_total = attend_forward(queries, keys, values, keep_mask)
        attended = (
            (attended * query_valid[:, None, None]).astype(bf16).reshape(chip_tokens, q_width)
        )
        stream_mid = stream + wires.chip_sum(dot(attended, out_here, ((1,), (1,))))
        scale_two = norm_scale(stream_mid)
        normed_two = (stream_mid * scale_two * gain_rows[1]).astype(bf16)
        blocks = wires.token_gather(normed_two)
        block_gates, up_gates, block_outs = [], [], []
        for block, route_rows in zip(blocks, block_routes):
            gates = expert_gates(block, router, route_rows, expert_ids)[0]
            gate = jnp.sum(jnp.where(my_expert, gates, 0.0), axis=1, keepdims=True)
            up_gate = dot(block, gate_up_here, ((1,), (0,)))
            hidden = (jax.nn.silu(up_gate[:, :ff_width]) * up_gate[:, ff_width:]).astype(bf16)
            out = dot(hidden, down_here, ((1,), (0,)))
            block_gates.append(gate)
            up_gates.append(up_gate)
            block_outs.append((out * gate).astype(bf16))
        stored.append(
            (
                stream,
                stream_mid,
                scale_one,
                scale_two,
                normed_one,
                normed_two,
                queries,
                keys,
                values,
                log_total,
                attended,
                blocks,
                block_gates,
                up_gates,
            )
        )
        stream = stream_mid + wires.token_scatter(block_outs)
    layer_out = stream.astype(bf16)
    stream_grad = cotangent.astype(f32)
    grad_layers = []
    for layer_index in range(layer_count - 1, -1, -1):
        (
            stream,
            stream_mid,
            scale_one,
            scale_two,
            normed_one,
            normed_two,
            queries,
            keys,
            values,
            log_total,
            attended,
            blocks,
            block_gates,
            up_gates,
        ) = stored[layer_index]
        gain_rows, qkv_here, out_here, router = held_weights[layer_index]
        gate_up_here = w_gate_up[layer_index, 0]
        down_here = w_down[layer_index, 0]
        grad_blocks = wires.token_gather(stream_grad.astype(bf16))
        pair_grads, hiddens, in_grads, gate_grads = [], [], [], []
        for grad_block, gate, up_gate in zip(grad_blocks, block_gates, up_gates):
            gate_part = up_gate[:, :ff_width]
            up_part = up_gate[:, ff_width:]
            sigmoid_gate = jax.nn.sigmoid(gate_part)
            activated = gate_part * sigmoid_gate
            hidden = activated * up_part
            back = dot(grad_block, down_here, ((1,), (1,)))
            gate_grads.append(jnp.sum(hidden * back, axis=1))
            hidden_grad = back * gate
            pair_grad = jnp.concatenate(
                [
                    hidden_grad * up_part * sigmoid_gate * (1.0 + gate_part * (1.0 - sigmoid_gate)),
                    hidden_grad * activated,
                ],
                axis=1,
            ).astype(bf16)
            pair_grads.append(pair_grad)
            hiddens.append((hidden * gate).astype(bf16))
            in_grads.append(dot(pair_grad, gate_up_here, ((1,), (1,))).astype(bf16))
        gate_rows = jnp.zeros((wires.dp_count, tok_rows), f32)
        for owners, gate_grad in zip(wires.token_owner(), gate_grads):
            for place, owner in enumerate(owners):
                gate_rows = lax.dynamic_update_slice(
                    gate_rows, gate_grad[place * tok_rows :][None, :tok_rows], (owner, 0)
                )
        gate_rows = lax.all_to_all(gate_rows, "dp", split_axis=0, concat_axis=0, tiled=True)
        normed_grad = wires.token_scatter(in_grads)
        pair_all = jnp.concatenate(pair_grads, axis=0)
        gate_up_grad = dot(jnp.concatenate(blocks, axis=0), pair_all, ((0,), (0,))).astype(bf16)
        down_grad = dot(
            jnp.concatenate(hiddens, axis=0), jnp.concatenate(grad_blocks, axis=0), ((0,), (0,))
        ).astype(bf16)
        gate_up_sum = wires.seq_scatter(gate_up_grad)
        down_sum = wires.seq_scatter(down_grad)
        gates, named = expert_gates(normed_two, router, routes, expert_ids)
        gate_grad = jnp.where(named, gate_rows.T, 0.0)
        logit_grad = gates * (gate_grad - jnp.sum(gates * gate_grad, axis=1, keepdims=True))
        logit_grad = logit_grad.astype(bf16)
        router_grad = dot(normed_two, logit_grad, ((0,), (0,)))
        normed_grad = normed_grad + dot(logit_grad, router, ((1,), (1,)))
        gain_two_grad, mid_grad = norm_back(stream_mid, scale_two, gain_rows[1], normed_grad)
        mid_grad = stream_grad + mid_grad
        attn_grad = wires.chip_rows(mid_grad.astype(bf16))
        head_grad = dot(attn_grad, out_here, ((1,), (0,))) * query_valid[:, None]
        head_grad = head_grad.astype(bf16).reshape(chip_tokens, heads_here, HEAD)
        out_grad = dot(attn_grad, attended, ((0,), (0,))).astype(bf16)
        query_grad, key_grad, value_grad = attend_backward(
            queries, keys, values, head_grad, log_total, keep_mask
        )
        pair_sums = jnp.concatenate([key_grad, value_grad], axis=1)
        own_grad = pair_sums[depth * chip_tokens :]
        for step in range(depth, 0, -1):
            first = (depth - step) * chip_tokens
            part = pair_sums[first : first + chip_tokens].astype(bf16)
            own_grad = own_grad + wires.chips_on(part, -step).astype(f32)
        query_lin = rope_turn(query_grad, position, -1.0).reshape(chip_tokens, q_width)
        key_lin = rope_turn(own_grad[:, None, :HEAD], position, -1.0)[:, 0]
        mixed_grad = jnp.concatenate([query_lin, key_lin, own_grad[:, HEAD:]], axis=1).astype(bf16)
        normed_one_grad = wires.chip_sum(dot(mixed_grad, qkv_here, ((1,), (1,))))
        gain_one_grad, front_grad = norm_back(stream, scale_one, gain_rows[0], normed_one_grad)
        stream_grad = mid_grad + front_grad
        qkv_grad = dot(normed_one, mixed_grad, ((0,), (0,))).astype(bf16)
        small = jnp.concatenate([router_grad, jnp.stack([gain_one_grad, gain_two_grad]).T], axis=1)
        small = jnp.pad(small, ((0, 0), (0, small_width - small.shape[1]))).astype(bf16)

        def shared(value):
            rows = value.shape[0] // 2
            kept, sent = wires.picked(core, value.reshape(2, rows, value.shape[1]), 0)
            return kept, wires.to_core(sent.astype(bf16)).astype(f32)

        back_own, back_other = shared(wires.chip_scatter(out_grad))
        front_own, front_other = shared(
            wires.chip_scatter(jnp.concatenate([qkv_grad, small], axis=1))
        )
        out_sum = wires.ordered(core, back_own, back_other, 1)
        out_sum = out_sum.reshape(out_sum.shape[0], HEADS * HEAD).T
        small_sum = (front_own + front_other)[:, qkv_width:]
        qkv_pair = wires.ordered(core, front_own[:, :qkv_width], front_other[:, :qkv_width], 1)
        rows = qkv_pair.shape[0]
        qkv_sum = jnp.concatenate(
            [
                qkv_pair[:, :, :q_width].reshape(rows, HEADS * HEAD),
                qkv_pair[:, :, q_width : q_width + HEAD].reshape(rows, KV_HEADS * HEAD),
                qkv_pair[:, :, q_width + HEAD :].reshape(rows, KV_HEADS * HEAD),
            ],
            axis=1,
        )
        gain_sum = small_sum[:, expert_count : expert_count + 2].T
        router_sum = small_sum[:, :expert_count]
        grad_layers.append((gain_sum, qkv_sum, out_sum, router_sum, gate_up_sum, down_sum))
    grad_layers = grad_layers[::-1]
    stacked = [jnp.stack([grad_entry[member] for grad_entry in grad_layers]) for member in range(6)]
    return (
        layer_out,
        stream_grad,
        stacked[0],
        stacked[1],
        stacked[2],
        stacked[3],
        stacked[4][:, None],
        stacked[5][:, None],
    )


def solution(mesh):
    return jax.shard_map(
        per_device,
        mesh=mesh,
        in_specs=(
            P(("dp", "seq"), None),
            P(("dp", "seq"), None),
            P(),
            P(("dp", "seq"), None),
            P(None, None, ("dp", "seq")),
            P(None, ("dp", "seq"), None),
            P(None, None, ("dp", "seq")),
            P(None, ("dp", "seq"), None),
            P(None, "dp", None, None),
            P(None, "dp", None, None),
        ),
        out_specs=(
            P(("dp", "seq"), None),
            P(("dp", "seq"), None),
            P(None, None, ("dp", "seq")),
            P(None, ("dp", "seq"), None),
            P(None, None, ("dp", "seq")),
            P(None, ("dp", "seq"), None),
            P(None, "dp", "seq", None),
            P(None, "dp", "seq", None),
        ),
        check_vma=False,
    )
```

```python
import jax
import jax.numpy as jnp
from jax import lax
from jax.experimental import pallas as pl
from jax.experimental.pallas import tpu as pltpu
from jax.sharding import PartitionSpec as P

HEADS = 12
KV_HEADS = 2
HEAD = 128
WINDOW = 1024
SEQ_LEN = 8192


norm_eps = 1e-06
rope_base = 1000000.0


ALL = ("dp", "seq")
CORES = 2
LINE = 4
HIDDEN_SCORE = -1e30
KERNEL_BYTES = 24 * 2**20
f32 = jnp.float32
bf16 = jnp.bfloat16


def dot(left, right, dims):
    return lax.dot_general(left, right, (dims, ((), ())), preferred_element_type=f32)


class Wires:
    def __init__(self):
        self.dp_count = lax.axis_size("dp")
        self.seq_count = lax.axis_size("seq")
        self.pairs = self.seq_count // CORES
        self.length = self.dp_count // 2
        dp_index = lax.axis_index("dp")
        seq_index = lax.axis_index("seq")
        self.dp_index = dp_index
        self.line = dp_index // 2
        self.side = dp_index % 2
        self.pair = seq_index // CORES
        self.core = seq_index % CORES
        self.chip = dp_index * self.pairs + self.pair
        self.chips = self.dp_count * self.pairs
        self.by_line = self.length == LINE and self.pairs == 2

    def to_core(self, value):
        return lax.ppermute(value, "seq", [(i, i ^ 1) for i in range(self.seq_count)])

    def to_pair(self, value):
        return lax.ppermute(value, "seq", [(i, i ^ 2) for i in range(self.seq_count)])

    def to_side(self, value):
        return lax.ppermute(value, "dp", [(i, i ^ 1) for i in range(self.dp_count)])

    def along(self, value, steps):
        count = self.dp_count
        return lax.ppermute(value, "dp", [(i, (i + 2 * steps) % count) for i in range(count)])

    def chips_on(self, value, steps):
        count = self.dp_count * self.seq_count
        offset = steps * CORES
        first, last = (max(0, -offset), min(count, count - offset))
        return lax.ppermute(value, ALL, [(i, i + offset) for i in range(first, last)])

    def ordered(self, flag, own, other, axis):
        return jnp.stack(
            [jnp.where(flag == 0, own, other), jnp.where(flag == 0, other, own)], axis=axis
        )

    def token_gather(self, value):
        if not self.by_line:
            return [lax.all_gather(value, "dp", axis=0, tiled=True)]
        side = self.to_side(value)
        one, three = self.along(value, 1), self.along(value, 3)
        held, one, three = lax.optimization_barrier((value, one, three))
        two = self.along(held, 2)
        odd = jnp.concatenate([one, three], axis=0)
        return [
            jnp.concatenate([value, side], axis=0),
            jnp.concatenate([odd, self.to_side(odd)], axis=0),
            jnp.concatenate([two, self.to_side(two)], axis=0),
        ]

    def token_scatter(self, blocks):
        if not self.by_line:
            return lax.psum_scatter(blocks[0], "dp", scatter_dimension=0, tiled=True).astype(f32)
        rows = blocks[0].shape[0] // 2

        def folded(block):
            half = block.shape[0] // 2
            return block[:half].astype(f32) + self.to_side(block[half:]).astype(f32)

        odd = folded(blocks[1]).astype(bf16)
        one, three = self.along(odd[:rows], -1), self.along(odd[rows:], -3)
        two = folded(blocks[2]).astype(bf16)
        held, one, three = lax.optimization_barrier((two, one, three))
        two = self.along(held, -2)
        return folded(blocks[0]) + one.astype(f32) + three.astype(f32) + two.astype(f32)

    def token_owner(self):
        if not self.by_line:
            return [list(range(self.dp_count))]
        place = [lax.rem(self.line - k + self.length, self.length) * 2 for k in range(LINE)]
        return [
            [place[k] + side for side in (self.side, 1 - self.side) for k in members]
            for members in ((0,), (1, 3), (2,))
        ]

    def core_groups(self):
        count = self.dp_count * self.seq_count
        return [list(range(core, count, CORES)) for core in range(CORES)]

    def chip_gather(self, one, two):
        rows, width = one.shape
        if not self.by_line:
            whole = lax.all_gather(
                jnp.concatenate([one, two], axis=1),
                ALL,
                axis=0,
                tiled=True,
                axis_index_groups=self.core_groups(),
            )
            return whole[:, :width], whole[:, width:]
        block = jnp.concatenate([one, two], axis=1)
        lines = jnp.zeros((LINE,) + block.shape, block.dtype)
        for k in range(LINE):
            piece = block if k == 0 else self.along(block, k)
            place = lax.rem(self.line - k + self.length, self.length)
            lines = lax.dynamic_update_slice(lines, piece[None], (place, 0, 0))
        one, two = lines[:, :, :width], lines[:, :, width:]
        one = self.ordered(self.side, one, self.to_side(one), 1)
        two = self.ordered(self.pair, two, self.to_pair(two), 1)
        one = self.ordered(self.pair, one, self.to_pair(one), 2)
        two = self.ordered(self.side, two, self.to_side(two), 1)
        return one.reshape(self.chips * rows, -1), two.reshape(self.chips * rows, -1)

    def picked(self, flag, stacked, axis):
        first, second = (
            lax.index_in_dim(stacked, 0, axis, keepdims=False),
            lax.index_in_dim(stacked, 1, axis, keepdims=False),
        )
        return jnp.where(flag == 0, first, second), jnp.where(flag == 0, second, first)

    def chip_scatter(self, one, two):
        width = one.shape[1]
        rows = one.shape[0] // self.chips
        if not self.by_line:
            total = lax.psum_scatter(
                jnp.concatenate([one, two], axis=1),
                ALL,
                scatter_dimension=0,
                tiled=True,
                axis_index_groups=self.core_groups(),
            ).astype(f32)
            return total[:, :width], total[:, width:]

        def step(flag, stacked, axis, move):
            kept, sent = self.picked(flag, stacked, axis)
            return (kept.astype(f32) + move(sent).astype(f32)).astype(bf16)

        one = one.reshape(LINE, 2, 2, rows, -1)
        two = two.reshape(LINE, 2, 2, rows, -1)
        one = step(self.pair, one, 2, self.to_pair)
        two = step(self.side, two, 1, self.to_side)
        one = step(self.side, one, 1, self.to_side)
        two = step(self.pair, two, 1, self.to_pair)
        both = jnp.concatenate([one, two], axis=2)
        total = None
        for k in range(LINE):
            place = lax.rem(self.line - k + self.length, self.length)
            piece = lax.dynamic_index_in_dim(both, place, 0, keepdims=False)
            piece = (piece if k == 0 else self.along(piece, -k)).astype(f32)
            total = piece if k == 0 else total + piece
        return total[:, :width], total[:, width:]

    def chip_rows(self, value):
        return jnp.concatenate([value, self.to_core(value)], axis=0)

    def chip_sum(self, value):
        rows = value.shape[0] // 2
        return value[:rows] + self.to_core(value[rows:].astype(bf16)).astype(f32)

    def seq_scatter(self, value):
        rows, columns = value.shape
        if self.pairs != 2:
            return lax.psum_scatter(value, "seq", scatter_dimension=0, tiled=True).astype(f32)
        piece = value.reshape(2, 2, rows // 4, columns)
        kept, sent = self.picked(self.core, piece, 1)
        piece = (kept.astype(f32) + self.to_core(sent).astype(f32)).astype(bf16)
        kept, sent = self.picked(self.pair, piece, 0)
        return kept.astype(f32) + self.to_pair(sent).astype(f32)


def doc_labels(token_index, doc_lengths, seq_length):
    doc_total = doc_lengths.shape[1]
    doc_ends = jnp.cumsum(doc_lengths, axis=1)
    clamped = jnp.maximum(token_index, 0)
    seq_number = clamped // seq_length
    position = clamped % seq_length
    seq_pick = seq_number[:, None] == jnp.arange(doc_lengths.shape[0], dtype=jnp.int32)[None, :]
    token_ends = jnp.sum(jnp.where(seq_pick[:, :, None], doc_ends[None, :, :], 0), axis=1)
    doc_number = jnp.sum((position[:, None] >= token_ends).astype(jnp.int32), axis=1)
    doc_label = jnp.where(token_index >= 0, seq_number * doc_total + doc_number, -1)
    is_valid = (doc_number < doc_total - 1).astype(jnp.float32)
    return (doc_label, is_valid, position)


def turn_tables(position):
    half_width = HEAD // 2
    frequency = rope_base ** (-jnp.arange(half_width, dtype=jnp.float32) * 2.0 / HEAD)
    angles = position.astype(jnp.float32)[:, None] * frequency[None, :]
    cosine, sine = jnp.cos(angles), jnp.sin(angles)
    return (
        jnp.concatenate([cosine, cosine], axis=1),
        jnp.concatenate([-sine, sine], axis=1),
    )


def rope_turn(vectors, turn, direction):
    half_width = HEAD // 2
    swapped = jnp.concatenate([vectors[:, half_width:], vectors[:, :half_width]], axis=1)
    return vectors * turn[0] + swapped * (direction * turn[1])


def norm_scale(stream):
    return lax.rsqrt(jnp.mean(stream * stream, axis=-1, keepdims=True) + norm_eps)


def norm_back(stream, scale, gain, out_grad):
    gain_grad = jnp.sum(out_grad * stream * scale, axis=0)
    scaled_grad = out_grad * gain
    stream_grad = scale * scaled_grad - stream * scale**3 * jnp.mean(
        scaled_grad * stream, axis=-1, keepdims=True
    )
    return (gain_grad, stream_grad)


def keep_rule(query_index, key_index, query_label, key_label):
    distance = query_index[:, None] - key_index[None, :]
    same_doc = query_label[:, None] == key_label[None, :]
    return same_doc & (distance >= 0) & (distance < WINDOW)


def turned(vectors, cosine, sine):
    return vectors * cosine + pltpu.roll(vectors, HEAD // 2, 1) * sine


def score_probs(queries, keys, bias):
    scores = dot(queries, keys, ((1,), (1,))) * HEAD ** (-0.5) + bias
    weights = jnp.exp(scores - jnp.max(scores, axis=1, keepdims=True))
    return weights * (1.0 / jnp.sum(weights, axis=1, keepdims=True))


def forward_kernel(mixed, keys, values, bias, cosine, sine, valid, attended, queries):
    turned_queries = turned(mixed[...], cosine[...], sine[...]).astype(bf16)
    queries[...] = turned_queries
    prob_rows = score_probs(turned_queries, keys[...], bias[...]).astype(bf16)
    out = dot(prob_rows, values[...], ((1,), (0,)))
    attended[...] = (out * valid[...]).astype(bf16)


def attend_forward(mixed, table, bias, turn, valid):
    rows = mixed.shape[0]
    key_rows = table.shape[0]
    heads = HEADS // CORES
    per_head = pl.BlockSpec((rows, HEAD), lambda h: (0, h))
    fixed = pl.BlockSpec((rows, HEAD), lambda h: (0, 0))
    return pl.pallas_call(
        forward_kernel,
        grid=(heads,),
        in_specs=[
            per_head,
            pl.BlockSpec((key_rows, HEAD), lambda h: (0, 0)),
            pl.BlockSpec((key_rows, HEAD), lambda h: (0, 1)),
            pl.BlockSpec((rows, key_rows), lambda h: (0, 0)),
            fixed,
            fixed,
            fixed,
        ],
        out_specs=[per_head, per_head],
        out_shape=[jax.ShapeDtypeStruct((rows, heads * HEAD), bf16)] * 2,
        compiler_params=pltpu.CompilerParams(vmem_limit_bytes=KERNEL_BYTES),
        cost_estimate=pl.CostEstimate(
            flops=4 * heads * rows * key_rows * HEAD,
            bytes_accessed=4 * rows * key_rows + 8 * rows * heads * HEAD,
            transcendentals=heads * rows * key_rows,
        ),
        name="attend_forward",
    )(mixed, table, table, bias, turn[0], turn[1], valid)


def backward_kernel(
    queries, head_grad, keys, values, bias, cosine, sine, query_grad, key_grad, value_grad
):
    scale = HEAD ** (-0.5)

    @pl.when(pl.program_id(0) == 0)
    def _():
        key_grad[...] = jnp.zeros_like(key_grad)
        value_grad[...] = jnp.zeros_like(value_grad)

    prob_rows = score_probs(queries[...], keys[...], bias[...])
    prob_grad = dot(head_grad[...], values[...], ((1,), (1,)))
    row_dot = jnp.sum(prob_rows * prob_grad, axis=1, keepdims=True)
    score_grad = (prob_rows * (prob_grad - row_dot)).astype(bf16)
    grad = dot(score_grad, keys[...], ((1,), (0,))) * scale
    query_grad[...] = turned(grad, cosine[...], -sine[...]).astype(bf16)
    key_grad[...] += dot(score_grad, queries[...], ((0,), (0,))) * scale
    value_grad[...] += dot(prob_rows.astype(bf16), head_grad[...], ((0,), (0,)))


def attend_backward(queries, head_grad, table, bias, turn):
    rows = queries.shape[0]
    key_rows = table.shape[0]
    heads = HEADS // CORES
    per_head = pl.BlockSpec((rows, HEAD), lambda h: (0, h))
    fixed = pl.BlockSpec((rows, HEAD), lambda h: (0, 0))
    table_grad = pl.BlockSpec((key_rows, HEAD), lambda h: (0, 0))
    return pl.pallas_call(
        backward_kernel,
        grid=(heads,),
        in_specs=[
            per_head,
            per_head,
            pl.BlockSpec((key_rows, HEAD), lambda h: (0, 0)),
            pl.BlockSpec((key_rows, HEAD), lambda h: (0, 1)),
            pl.BlockSpec((rows, key_rows), lambda h: (0, 0)),
            fixed,
            fixed,
        ],
        out_specs=[per_head, table_grad, table_grad],
        out_shape=[
            jax.ShapeDtypeStruct((rows, heads * HEAD), bf16),
            jax.ShapeDtypeStruct((key_rows, HEAD), f32),
            jax.ShapeDtypeStruct((key_rows, HEAD), f32),
        ],
        compiler_params=pltpu.CompilerParams(vmem_limit_bytes=KERNEL_BYTES),
        cost_estimate=pl.CostEstimate(
            flops=10 * heads * rows * key_rows * HEAD,
            bytes_accessed=4 * rows * key_rows + 8 * rows * heads * HEAD,
            transcendentals=heads * rows * key_rows,
        ),
        name="attend_backward",
    )(queries, head_grad, table, table, bias, turn[0], turn[1])


def expert_gates(normed, router, routes, expert_ids):
    logits = dot(normed, router, ((1,), (0,)))
    named = jnp.any(routes[:, :, None] == expert_ids[None, None, :], axis=1)
    top = jnp.max(jnp.where(named, logits, -jnp.inf), axis=1, keepdims=True)
    weights = jnp.where(named, jnp.exp(logits - top), 0.0)
    return weights / jnp.sum(weights, axis=1, keepdims=True), named


def per_device(
    activations,
    cotangent,
    doc_lengths,
    routes,
    norm_gains,
    w_qkv,
    w_out,
    w_router,
    w_gate_up,
    w_down,
):
    wires = Wires()
    tok_rows, model_width = activations.shape
    layer_count = w_qkv.shape[0]
    heads_here = HEADS // CORES
    q_width = heads_here * HEAD
    qkv_width = q_width + 2 * HEAD
    ff_width = w_down.shape[2]
    expert_count = w_router.shape[2]
    chip_tokens = CORES * tok_rows
    device_count = wires.dp_count * wires.seq_count
    seq_length = min(SEQ_LEN, tok_rows * device_count)
    depth = min(-(-(WINDOW - 1) // chip_tokens), wires.chips - 1)
    core = wires.core

    def chip_index_of(first_chip, chips):
        block = first_chip + jnp.arange(chips, dtype=jnp.int32)
        order = jnp.stack([core, 1 - core]).astype(jnp.int32)
        start = block[:, None] * chip_tokens + order[None, :] * tok_rows
        return (start[:, :, None] + jnp.arange(tok_rows, dtype=jnp.int32)).reshape(-1)

    query_index = chip_index_of(wires.chip, 1)
    key_index = chip_index_of(wires.chip - depth, depth + 1)
    query_label, query_valid, position = doc_labels(query_index, doc_lengths, seq_length)
    key_label = doc_labels(key_index, doc_lengths, seq_length)[0]
    bias = jnp.where(
        keep_rule(query_index, key_index, query_label, key_label), 0.0, HIDDEN_SCORE
    ).astype(f32)
    turn = turn_tables(position)
    valid = jnp.broadcast_to(query_valid[:, None], (chip_tokens, HEAD))
    expert_ids = jnp.arange(expert_count, dtype=jnp.int32)
    my_expert = (expert_ids == wires.dp_index)[None, :]
    route_names = jnp.pad(routes.astype(bf16), ((0, 0), (0, 128 - routes.shape[1])))
    small_width = -(-(expert_count + 2) // 128) * 128

    def packed_weights(layer_index):
        out_rows = w_out[layer_index].T
        qkv = w_qkv[layer_index]
        small = jnp.concatenate([w_router[layer_index], norm_gains[layer_index].T], axis=1)
        small = jnp.pad(small, ((0, 0), (0, small_width - small.shape[1])))
        fronts, backs = [], []
        for c in range(CORES):
            fronts.append(
                jnp.concatenate(
                    [
                        qkv[:, c * q_width : (c + 1) * q_width],
                        qkv[:, HEADS * HEAD + c * HEAD :][:, :HEAD],
                        qkv[:, (HEADS + KV_HEADS + c) * HEAD :][:, :HEAD],
                        small,
                    ],
                    axis=1,
                )
            )
            backs.append(out_rows[:, c * q_width : (c + 1) * q_width])
        def per_chip(first, second):
            kept = jnp.where(core == 0, first, second)
            sent = jnp.where(core == 0, second, first)
            block = wires.ordered(core, kept, wires.to_core(sent), 0)
            return block.reshape(2 * kept.shape[0], kept.shape[1])

        return per_chip(*fronts), per_chip(*backs)

    packed = [packed_weights(layer_index) for layer_index in range(layer_count)]
    cut = (q_width // 2) // 128 * 128 + 256
    fronts = [
        jnp.concatenate(wires.chip_gather(packed[0][0][:, :cut], packed[0][0][:, cut:]), axis=1)
    ]
    rest_front = jnp.concatenate([front for front, _ in packed[1:]], axis=1)
    rest_back = jnp.concatenate([back for _, back in packed], axis=1)
    rest_front, rest_back, fronts[0] = lax.optimization_barrier((rest_front, rest_back, fronts[0]))
    rest_front, rest_back = wires.chip_gather(rest_front, rest_back)
    front_width = qkv_width + small_width
    held_weights = []
    for layer_index in range(layer_count):
        if layer_index > 0:
            fronts.append(rest_front[:, (layer_index - 1) * front_width :][:, :front_width])
        front = fronts[layer_index]
        back = rest_back[:, layer_index * q_width : (layer_index + 1) * q_width]
        small = front[:, qkv_width:]
        held_weights.append(
            (
                small[:, expert_count : expert_count + 2].astype(f32).T,
                front[:, :qkv_width],
                back,
                small[:, :expert_count],
            )
        )
    stream = activations.astype(f32)
    stored = []
    for layer_index in range(layer_count):
        gain_rows, qkv_here, out_here, router = held_weights[layer_index]
        gate_up_here = w_gate_up[layer_index, 0]
        down_here = w_down[layer_index, 0]
        scale_one = norm_scale(stream)
        normed_one = wires.chip_rows((stream * scale_one * gain_rows[0]).astype(bf16))
        mixed = dot(normed_one, qkv_here, ((1,), (0,)))
        own_keys = rope_turn(mixed[:, q_width : q_width + HEAD], turn, 1.0)
        own_pair = jnp.concatenate([own_keys, mixed[:, q_width + HEAD :]], axis=1).astype(bf16)
        table = jnp.concatenate(
            [wires.chips_on(own_pair, step) for step in range(depth, 0, -1)] + [own_pair], axis=0
        )
        attended, queries = attend_forward(mixed, table, bias, turn, valid)
        stream_mid = stream + wires.chip_sum(dot(attended, out_here, ((1,), (1,))))
        scale_two = norm_scale(stream_mid)
        normed_two = (stream_mid * scale_two * gain_rows[1]).astype(bf16)
        if layer_index == 0:
            blocks = wires.token_gather(jnp.concatenate([normed_two, route_names], axis=1))
            block_routes = [
                block[:, model_width : model_width + routes.shape[1]].astype(jnp.int32)
                for block in blocks
            ]
            blocks = [block[:, :model_width] for block in blocks]
        else:
            blocks = wires.token_gather(normed_two)
        block_gates, up_gates, block_outs = [], [], []
        for block, route_rows in zip(blocks, block_routes):
            gates = expert_gates(block, router, route_rows, expert_ids)[0]
            gate = jnp.sum(jnp.where(my_expert, gates, 0.0), axis=1, keepdims=True)
            up_gate = dot(block, gate_up_here, ((1,), (0,)))
            hidden = (jax.nn.silu(up_gate[:, :ff_width]) * up_gate[:, ff_width:]).astype(bf16)
            out = dot(hidden, down_here, ((1,), (0,)))
            block_gates.append(gate)
            up_gates.append(up_gate)
            block_outs.append((out * gate).astype(bf16))
        stored.append(
            (
                stream,
                stream_mid,
                scale_one,
                scale_two,
                normed_one,
                normed_two,
                queries,
                table,
                attended,
                blocks,
                block_gates,
                up_gates,
            )
        )
        stream = stream_mid + wires.token_scatter(block_outs)
    layer_out = stream.astype(bf16)
    stream_grad = cotangent.astype(f32)
    grad_layers = []
    for layer_index in range(layer_count - 1, -1, -1):
        (
            stream,
            stream_mid,
            scale_one,
            scale_two,
            normed_one,
            normed_two,
            queries,
            table,
            attended,
            blocks,
            block_gates,
            up_gates,
        ) = stored[layer_index]
        gain_rows, qkv_here, out_here, router = held_weights[layer_index]
        gate_up_here = w_gate_up[layer_index, 0]
        down_here = w_down[layer_index, 0]
        grad_blocks = wires.token_gather(stream_grad.astype(bf16))
        pair_grads, hiddens, in_grads, gate_grads = [], [], [], []
        for grad_block, gate, up_gate in zip(grad_blocks, block_gates, up_gates):
            gate_part = up_gate[:, :ff_width]
            up_part = up_gate[:, ff_width:]
            sigmoid_gate = jax.nn.sigmoid(gate_part)
            activated = gate_part * sigmoid_gate
            hidden = activated * up_part
            back = dot(grad_block, down_here, ((1,), (1,)))
            gate_grads.append(jnp.sum(hidden * back, axis=1))
            hidden_grad = back * gate
            pair_grad = jnp.concatenate(
                [
                    hidden_grad * up_part * sigmoid_gate * (1.0 + gate_part * (1.0 - sigmoid_gate)),
                    hidden_grad * activated,
                ],
                axis=1,
            ).astype(bf16)
            pair_grads.append(pair_grad)
            hiddens.append((hidden * gate).astype(bf16))
            in_grads.append(dot(pair_grad, gate_up_here, ((1,), (1,))).astype(bf16))
        gate_rows = jnp.zeros((wires.dp_count, tok_rows), f32)
        for owners, gate_grad in zip(wires.token_owner(), gate_grads):
            for place, owner in enumerate(owners):
                gate_rows = lax.dynamic_update_slice(
                    gate_rows, gate_grad[place * tok_rows :][None, :tok_rows], (owner, 0)
                )
        gate_rows = lax.all_to_all(gate_rows, "dp", split_axis=0, concat_axis=0, tiled=True)
        normed_grad = wires.token_scatter(in_grads)
        pair_all = jnp.concatenate(pair_grads, axis=0)
        gate_up_grad = dot(jnp.concatenate(blocks, axis=0), pair_all, ((0,), (0,))).astype(bf16)
        down_grad = dot(
            jnp.concatenate(hiddens, axis=0), jnp.concatenate(grad_blocks, axis=0), ((0,), (0,))
        ).astype(bf16)
        gate_up_sum = wires.seq_scatter(gate_up_grad)
        down_sum = wires.seq_scatter(down_grad)
        gates, named = expert_gates(normed_two, router, routes, expert_ids)
        gate_grad = jnp.where(named, gate_rows.T, 0.0)
        logit_grad = gates * (gate_grad - jnp.sum(gates * gate_grad, axis=1, keepdims=True))
        logit_grad = logit_grad.astype(bf16)
        router_grad = dot(normed_two, logit_grad, ((0,), (0,)))
        normed_grad = normed_grad + dot(logit_grad, router, ((1,), (1,)))
        gain_two_grad, mid_grad = norm_back(stream_mid, scale_two, gain_rows[1], normed_grad)
        mid_grad = stream_grad + mid_grad
        attn_grad = wires.chip_rows(mid_grad.astype(bf16))
        head_grad = dot(attn_grad, out_here, ((1,), (0,))) * query_valid[:, None]
        head_grad = head_grad.astype(bf16)
        out_grad = dot(attn_grad, attended, ((0,), (0,))).astype(bf16)
        query_lin, key_grad, value_grad = attend_backward(queries, head_grad, table, bias, turn)
        pair_sums = jnp.concatenate([key_grad, value_grad], axis=1)
        own_grad = pair_sums[depth * chip_tokens :]
        for step in range(depth, 0, -1):
            first = (depth - step) * chip_tokens
            part = pair_sums[first : first + chip_tokens].astype(bf16)
            own_grad = own_grad + wires.chips_on(part, -step).astype(f32)
        key_lin = rope_turn(own_grad[:, :HEAD], turn, -1.0)
        mixed_grad = jnp.concatenate(
            [query_lin, key_lin.astype(bf16), own_grad[:, HEAD:].astype(bf16)], axis=1
        )
        normed_one_grad = wires.chip_sum(dot(mixed_grad, qkv_here, ((1,), (1,))))
        gain_one_grad, front_grad = norm_back(stream, scale_one, gain_rows[0], normed_one_grad)
        stream_grad = mid_grad + front_grad
        qkv_grad = dot(normed_one, mixed_grad, ((0,), (0,))).astype(bf16)
        small = jnp.concatenate([router_grad, jnp.stack([gain_one_grad, gain_two_grad]).T], axis=1)
        small = jnp.pad(small, ((0, 0), (0, small_width - small.shape[1]))).astype(bf16)

        def shared(value):
            rows = value.shape[0] // 2
            kept, sent = wires.picked(core, value.reshape(2, rows, value.shape[1]), 0)
            return kept, wires.to_core(sent.astype(bf16)).astype(f32)

        half = q_width // 2
        if layer_index > 0:
            front, back = wires.chip_scatter(jnp.concatenate([qkv_grad, small], axis=1), out_grad)
        else:
            back = jnp.concatenate(wires.chip_scatter(out_grad[:, :half], out_grad[:, half:]), axis=1)
            cut = qkv_width // 2
            front = jnp.concatenate(
                wires.chip_scatter(
                    qkv_grad[:, :cut], jnp.concatenate([qkv_grad[:, cut:], small], axis=1)
                ),
                axis=1,
            )
        back_own, back_other = shared(back)
        front_own, front_other = shared(front)
        out_sum = wires.ordered(core, back_own, back_other, 1)
        out_sum = out_sum.reshape(out_sum.shape[0], HEADS * HEAD).T
        small_sum = (front_own + front_other)[:, qkv_width:]
        qkv_pair = wires.ordered(core, front_own[:, :qkv_width], front_other[:, :qkv_width], 1)
        rows = qkv_pair.shape[0]
        qkv_sum = jnp.concatenate(
            [
                qkv_pair[:, :, :q_width].reshape(rows, HEADS * HEAD),
                qkv_pair[:, :, q_width : q_width + HEAD].reshape(rows, KV_HEADS * HEAD),
                qkv_pair[:, :, q_width + HEAD :].reshape(rows, KV_HEADS * HEAD),
            ],
            axis=1,
        )
        gain_sum = small_sum[:, expert_count : expert_count + 2].T
        router_sum = small_sum[:, :expert_count]
        grad_layers.append((gain_sum, qkv_sum, out_sum, router_sum, gate_up_sum, down_sum))
    grad_layers = grad_layers[::-1]
    stacked = [jnp.stack([grad_entry[member] for grad_entry in grad_layers]) for member in range(6)]
    return (
        layer_out,
        stream_grad,
        stacked[0],
        stacked[1],
        stacked[2],
        stacked[3],
        stacked[4][:, None],
        stacked[5][:, None],
    )


def solution(mesh):
    return jax.shard_map(
        per_device,
        mesh=mesh,
        in_specs=(
            P(("dp", "seq"), None),
            P(("dp", "seq"), None),
            P(),
            P(("dp", "seq"), None),
            P(None, None, ("dp", "seq")),
            P(None, ("dp", "seq"), None),
            P(None, None, ("dp", "seq")),
            P(None, ("dp", "seq"), None),
            P(None, "dp", None, None),
            P(None, "dp", None, None),
        ),
        out_specs=(
            P(("dp", "seq"), None),
            P(("dp", "seq"), None),
            P(None, None, ("dp", "seq")),
            P(None, ("dp", "seq"), None),
            P(None, None, ("dp", "seq")),
            P(None, ("dp", "seq"), None),
            P(None, "dp", "seq", None),
            P(None, "dp", "seq", None),
        ),
        check_vma=False,
    )
```

```python
import jax
import jax.numpy as jnp
from jax import lax
from jax.experimental import pallas as pl
from jax.experimental.pallas import tpu as pltpu
from jax.sharding import PartitionSpec as P

HEADS = 12
KV_HEADS = 2
HEAD = 128
WINDOW = 1024
SEQ_LEN = 8192


norm_eps = 1e-06
rope_base = 1000000.0


ALL = ("dp", "seq")
CORES = 2
LINE = 4
HIDDEN_SCORE = -1e30
KERNEL_BYTES = 24 * 2**20
f32 = jnp.float32
bf16 = jnp.bfloat16


def dot(left, right, dims):
    return lax.dot_general(left, right, (dims, ((), ())), preferred_element_type=f32)


def after(value, *events):
    there = None
    for event in events:
        if event is None:
            continue
        sample = lax.slice(event, (0,) * event.ndim, (1,) * event.ndim).reshape(())
        same = sample == sample
        there = same if there is None else there & same
    return value if there is None else jnp.where(there, value, jnp.zeros_like(value))


class Task:
    def __init__(self, legs):
        self.legs = legs
        self.marks = []
        self.result = None
        self.running = True
        self.go()

    def go(self, *events):
        if not self.running:
            return
        try:
            self.marks = self.legs.send(events) if self.marks else next(self.legs)
        except StopIteration as end:
            self.running = False
            self.marks = []
            self.result = end.value

    def finish(self):
        while self.running:
            self.go(*self.marks)
        return self.result


def phase(*tasks):
    events = [mark for task in tasks for mark in task.marks]
    for task in tasks:
        task.go(*events)


def place_of(stacked, index, axis):
    return lax.dynamic_index_in_dim(stacked, index, axis, keepdims=False)


class Wires:
    def __init__(self):
        self.dp_count = lax.axis_size("dp")
        self.seq_count = lax.axis_size("seq")
        self.pairs = self.seq_count // CORES
        self.length = self.dp_count // 2
        dp_index = lax.axis_index("dp")
        seq_index = lax.axis_index("seq")
        self.dp_index = dp_index
        self.line = dp_index // 2
        self.side = dp_index % 2
        self.pair = seq_index // CORES
        self.core = seq_index % CORES
        self.chip = dp_index * self.pairs + self.pair
        self.chips = self.dp_count * self.pairs
        self.by_line = self.length == LINE and self.pairs == 2

    def to_core(self, value):
        return lax.ppermute(value, "seq", [(i, i ^ 1) for i in range(self.seq_count)])

    def to_pair(self, value):
        return lax.ppermute(value, "seq", [(i, i ^ 2) for i in range(self.seq_count)])

    def to_side(self, value):
        return lax.ppermute(value, "dp", [(i, i ^ 1) for i in range(self.dp_count)])

    def along(self, value, steps):
        count = self.dp_count
        return lax.ppermute(value, "dp", [(i, (i + 2 * steps) % count) for i in range(count)])

    def chips_on(self, value, steps):
        count = self.dp_count * self.seq_count
        offset = steps * CORES
        first, last = (max(0, -offset), min(count, count - offset))
        return lax.ppermute(value, ALL, [(i, i + offset) for i in range(first, last)])

    def ordered(self, flag, own, other, axis):
        return jnp.stack(
            [jnp.where(flag == 0, own, other), jnp.where(flag == 0, other, own)], axis=axis
        )

    def token_gather(self, value, slowly=False):
        if not self.by_line:
            return [lax.all_gather(value, "dp", axis=0, tiled=True)]
        side = self.to_side(value)
        if slowly:
            events = yield [side]
            held = after(value, *events)
            one, three = self.along(held, 1), self.along(held, 3)
            events = yield [one, three]
            two = self.along(after(value, *events), 2)
            events = yield [two]
            odd = after(jnp.concatenate([one, three], axis=0), *events)
            odd_side = self.to_side(odd)
            events = yield [odd_side]
            two = after(two, *events)
        else:
            one, three = self.along(value, 1), self.along(value, 3)
            events = yield [side, one, three]
            odd = jnp.concatenate([one, three], axis=0)
            odd_side = self.to_side(odd)
            two = self.along(after(value, *events), 2)
            events = yield [odd_side, two]
            two = after(two, *[event for event in events if event is not two])
        two_side = self.to_side(two)
        events = yield [two_side]
        return [
            jnp.concatenate([value, side], axis=0),
            jnp.concatenate([odd, odd_side], axis=0),
            jnp.concatenate([two, two_side], axis=0),
        ]

    def token_scatter(self, blocks):
        if not self.by_line:
            return lax.psum_scatter(blocks[0], "dp", scatter_dimension=0, tiled=True).astype(f32)
        rows = blocks[0].shape[0] // 2
        odd = self.to_side(blocks[1][2 * rows :])
        events = yield [odd]
        odd = (blocks[1][: 2 * rows].astype(f32) + odd.astype(f32)).astype(bf16)
        one, three = self.along(odd[:rows], -1), self.along(odd[rows:], -3)
        two = self.to_side(after(blocks[2][rows:], *events))
        events = yield [one, three, two]
        two = (blocks[2][:rows].astype(f32) + two.astype(f32)).astype(bf16)
        two = self.along(after(two, *events), -2)
        side = self.to_side(after(blocks[0][rows:], *events))
        events = yield [two, side]
        total = blocks[0][:rows].astype(f32) + side.astype(f32)
        return total + one.astype(f32) + three.astype(f32) + two.astype(f32)

    def token_owner(self):
        if not self.by_line:
            return [list(range(self.dp_count))]
        place = [lax.rem(self.line - k + self.length, self.length) * 2 for k in range(LINE)]
        return [
            [place[k] + side for side in (self.side, 1 - self.side) for k in members]
            for members in ((0,), (1, 3), (2,))
        ]

    def key_gather(self, own, depth):
        earlier = [self.chips_on(own, step) for step in range(depth, 0, -1)]
        events = yield earlier
        return jnp.concatenate(earlier + [own], axis=0)

    def key_scatter(self, sums, depth):
        rows = sums.shape[0] // (depth + 1)
        earlier = [
            self.chips_on(sums[k * rows : (k + 1) * rows].astype(bf16), k - depth)
            for k in range(depth)
        ]
        events = yield earlier
        return sum(
            (value.astype(f32) for value in earlier), sums[depth * rows :]
        )

    def expert_sums(self, pairs):
        if not self.by_line:
            totals = [dot(inputs, grads, ((0,), (0,))).astype(bf16) for inputs, grads in pairs]
            return [
                lax.psum_scatter(total, "seq", scatter_dimension=0, tiled=True).astype(f32)
                for total in totals
            ]
        kept, crossed = [], []
        for inputs, grads in pairs:
            whole = dot(inputs, grads, ((0,), (0,))).astype(bf16)
            whole = whole.reshape(2, 2, whole.shape[0] // 4, -1)
            kept.append(place_of(whole, self.core, 1))
            crossed.append(self.to_core(place_of(whole, 1 - self.core, 1)))
        events = yield crossed

        def half(k, pair):
            return place_of(kept[k], pair, 0).astype(f32) + place_of(
                crossed[k], pair, 0
            ).astype(f32)

        others = [
            self.to_pair(after(half(k, 1 - self.pair).astype(bf16), *events))
            for k in range(len(pairs))
        ]
        events = yield others
        return [half(k, self.pair) + other.astype(f32) for k, other in enumerate(others)]

    def core_groups(self):
        count = self.dp_count * self.seq_count
        return [list(range(core, count, CORES)) for core in range(CORES)]

    def chip_gather_whole(self, block):
        return lax.all_gather(
            block, ALL, axis=0, tiled=True, axis_index_groups=self.core_groups()
        )

    def chip_scatter_whole(self, whole):
        return lax.psum_scatter(
            whole, ALL, scatter_dimension=0, tiled=True, axis_index_groups=self.core_groups()
        ).astype(f32)

    def chip_gather(self, one, two, slowly=False):
        rows, width = one.shape
        block = jnp.concatenate([one, two], axis=1)
        if not self.by_line:
            return self.chip_gather_whole(block)
        pieces = [block, self.along(block, 1), None, self.along(block, 3)]
        if slowly:
            events = yield [pieces[1], pieces[3]]
            pieces[2] = self.along(after(block, *events), 2)
            events = yield [pieces[2]]
        else:
            pieces[2] = self.along(block, 2)
            events = yield pieces[1:]
        lines = jnp.zeros((LINE,) + block.shape, block.dtype)
        for k, piece in enumerate(pieces):
            place = lax.rem(self.line - k + self.length, self.length)
            lines = lax.dynamic_update_slice(lines, piece[None], (place, 0, 0))
        lines = lines if not slowly else after(lines, *events)
        one, two = lines[:, :, :width], lines[:, :, width:]
        side, pair = self.to_side(one), self.to_pair(two)
        events = yield [side, pair]
        one = self.ordered(self.side, one, after(side, *events), 1)
        two = self.ordered(self.pair, two, after(pair, *events), 1)
        pair, side = self.to_pair(one), self.to_side(two)
        events = yield [pair, side]
        one = self.ordered(self.pair, one, pair, 2)
        two = self.ordered(self.side, two, side, 1)
        return jnp.concatenate(
            [part.reshape(self.chips * rows, -1) for part in (one, two)], axis=1
        )

    def chip_scatter(self, one, two, slowly=False):
        width = one.shape[1]
        rows = one.shape[0] // self.chips
        if not self.by_line:
            total = self.chip_scatter_whole(jnp.concatenate([one, two], axis=1))
            return total[:, :width], total[:, width:]

        def added(flag, stacked, axis, got, events):
            kept = place_of(stacked, flag, axis).astype(f32)
            return (kept + after(got, *events).astype(f32)).astype(bf16)

        one = one.reshape(LINE, 2, 2, rows, -1)
        two = two.reshape(LINE, 2, 2, rows, -1)
        got_one = self.to_pair(place_of(one, 1 - self.pair, 2))
        got_two = self.to_side(place_of(two, 1 - self.side, 1))
        events = yield [got_one, got_two]
        one = added(self.pair, one, 2, got_one, events)
        two = added(self.side, two, 1, got_two, events)
        got_one = self.to_side(place_of(one, 1 - self.side, 1))
        got_two = self.to_pair(place_of(two, 1 - self.pair, 1))
        events = yield [got_one, got_two]
        one = added(self.side, one, 1, got_one, events)
        two = added(self.pair, two, 1, got_two, events)
        both = jnp.concatenate([one, two], axis=2)
        pieces = [
            place_of(both, lax.rem(self.line - k + self.length, self.length), 0)
            for k in range(LINE)
        ]
        for k in (1, 3):
            pieces[k] = self.along(pieces[k], -k)
        if slowly:
            events = yield [pieces[1], pieces[3]]
            pieces[2] = self.along(after(pieces[2], *events), -2)
            events = yield [pieces[2]]
        else:
            pieces[2] = self.along(pieces[2], -2)
            events = yield pieces[1:]
        total = sum(piece.astype(f32) for piece in pieces)
        return total[:, :width], total[:, width:]

    def chip_rows(self, value):
        return jnp.concatenate([value, self.to_core(value)], axis=0)

    def chip_sum(self, value):
        rows = value.shape[0] // 2
        return value[:rows] + self.to_core(value[rows:].astype(bf16)).astype(f32)


def doc_labels(token_index, doc_lengths, seq_length):
    doc_total = doc_lengths.shape[1]
    doc_ends = jnp.cumsum(doc_lengths, axis=1)
    clamped = jnp.maximum(token_index, 0)
    seq_number = clamped // seq_length
    position = clamped % seq_length
    seq_pick = seq_number[:, None] == jnp.arange(doc_lengths.shape[0], dtype=jnp.int32)[None, :]
    token_ends = jnp.sum(jnp.where(seq_pick[:, :, None], doc_ends[None, :, :], 0), axis=1)
    doc_number = jnp.sum((position[:, None] >= token_ends).astype(jnp.int32), axis=1)
    doc_label = jnp.where(token_index >= 0, seq_number * doc_total + doc_number, -1)
    is_valid = (doc_number < doc_total - 1).astype(jnp.float32)
    return (doc_label, is_valid, position)


def turn_tables(position):
    half_width = HEAD // 2
    frequency = rope_base ** (-jnp.arange(half_width, dtype=jnp.float32) * 2.0 / HEAD)
    angles = position.astype(jnp.float32)[:, None] * frequency[None, :]
    cosine, sine = jnp.cos(angles), jnp.sin(angles)
    return (
        jnp.concatenate([cosine, cosine], axis=1),
        jnp.concatenate([-sine, sine], axis=1),
    )


def rope_turn(vectors, turn, direction):
    half_width = HEAD // 2
    swapped = jnp.concatenate([vectors[:, half_width:], vectors[:, :half_width]], axis=1)
    return vectors * turn[0] + swapped * (direction * turn[1])


def norm_scale(stream):
    return lax.rsqrt(jnp.mean(stream * stream, axis=-1, keepdims=True) + norm_eps)


def norm_back(stream, scale, gain, out_grad):
    gain_grad = jnp.sum(out_grad * stream * scale, axis=0)
    scaled_grad = out_grad * gain
    stream_grad = scale * scaled_grad - stream * scale**3 * jnp.mean(
        scaled_grad * stream, axis=-1, keepdims=True
    )
    return (gain_grad, stream_grad)


def keep_rule(query_index, key_index, query_label, key_label):
    distance = query_index[:, None] - key_index[None, :]
    same_doc = query_label[:, None] == key_label[None, :]
    return same_doc & (distance >= 0) & (distance < WINDOW)


def turned(vectors, cosine, sine):
    return vectors * cosine + pltpu.roll(vectors, HEAD // 2, 1) * sine


def score_probs(queries, keys, bias):
    scores = dot(queries, keys, ((1,), (1,))) * HEAD ** (-0.5) + bias
    weights = jnp.exp(scores - jnp.max(scores, axis=1, keepdims=True))
    return weights * (1.0 / jnp.sum(weights, axis=1, keepdims=True))


def forward_kernel(mixed, keys, values, bias, cosine, sine, valid, attended, queries):
    turned_queries = turned(mixed[...], cosine[...], sine[...]).astype(bf16)
    queries[...] = turned_queries
    prob_rows = score_probs(turned_queries, keys[...], bias[...]).astype(bf16)
    out = dot(prob_rows, values[...], ((1,), (0,)))
    attended[...] = (out * valid[...]).astype(bf16)


def attend_forward(mixed, table, bias, turn, valid):
    rows = mixed.shape[0]
    key_rows = table.shape[0]
    heads = HEADS // CORES
    per_head = pl.BlockSpec((rows, HEAD), lambda h: (0, h))
    fixed = pl.BlockSpec((rows, HEAD), lambda h: (0, 0))
    return pl.pallas_call(
        forward_kernel,
        grid=(heads,),
        in_specs=[
            per_head,
            pl.BlockSpec((key_rows, HEAD), lambda h: (0, 0)),
            pl.BlockSpec((key_rows, HEAD), lambda h: (0, 1)),
            pl.BlockSpec((rows, key_rows), lambda h: (0, 0)),
            fixed,
            fixed,
            fixed,
        ],
        out_specs=[per_head, per_head],
        out_shape=[jax.ShapeDtypeStruct((rows, heads * HEAD), bf16)] * 2,
        compiler_params=pltpu.CompilerParams(vmem_limit_bytes=KERNEL_BYTES),
        cost_estimate=pl.CostEstimate(
            flops=4 * heads * rows * key_rows * HEAD,
            bytes_accessed=4 * rows * key_rows + 8 * rows * heads * HEAD,
            transcendentals=heads * rows * key_rows,
        ),
        name="attend_forward",
    )(mixed, table, table, bias, turn[0], turn[1], valid)


def backward_kernel(
    queries, head_grad, keys, values, bias, cosine, sine, query_grad, key_grad, value_grad
):
    scale = HEAD ** (-0.5)

    @pl.when(pl.program_id(0) == 0)
    def _():
        key_grad[...] = jnp.zeros_like(key_grad)
        value_grad[...] = jnp.zeros_like(value_grad)

    prob_rows = score_probs(queries[...], keys[...], bias[...])
    prob_grad = dot(head_grad[...], values[...], ((1,), (1,)))
    row_dot = jnp.sum(prob_rows * prob_grad, axis=1, keepdims=True)
    score_grad = (prob_rows * (prob_grad - row_dot)).astype(bf16)
    grad = dot(score_grad, keys[...], ((1,), (0,))) * scale
    query_grad[...] = turned(grad, cosine[...], -sine[...]).astype(bf16)
    key_grad[...] += dot(score_grad, queries[...], ((0,), (0,))) * scale
    value_grad[...] += dot(prob_rows.astype(bf16), head_grad[...], ((0,), (0,)))


def attend_backward(queries, head_grad, table, bias, turn):
    rows = queries.shape[0]
    key_rows = table.shape[0]
    heads = HEADS // CORES
    per_head = pl.BlockSpec((rows, HEAD), lambda h: (0, h))
    fixed = pl.BlockSpec((rows, HEAD), lambda h: (0, 0))
    table_grad = pl.BlockSpec((key_rows, HEAD), lambda h: (0, 0))
    return pl.pallas_call(
        backward_kernel,
        grid=(heads,),
        in_specs=[
            per_head,
            per_head,
            pl.BlockSpec((key_rows, HEAD), lambda h: (0, 0)),
            pl.BlockSpec((key_rows, HEAD), lambda h: (0, 1)),
            pl.BlockSpec((rows, key_rows), lambda h: (0, 0)),
            fixed,
            fixed,
        ],
        out_specs=[per_head, table_grad, table_grad],
        out_shape=[
            jax.ShapeDtypeStruct((rows, heads * HEAD), bf16),
            jax.ShapeDtypeStruct((key_rows, HEAD), f32),
            jax.ShapeDtypeStruct((key_rows, HEAD), f32),
        ],
        compiler_params=pltpu.CompilerParams(vmem_limit_bytes=KERNEL_BYTES),
        cost_estimate=pl.CostEstimate(
            flops=10 * heads * rows * key_rows * HEAD,
            bytes_accessed=4 * rows * key_rows + 8 * rows * heads * HEAD,
            transcendentals=heads * rows * key_rows,
        ),
        name="attend_backward",
    )(queries, head_grad, table, table, bias, turn[0], turn[1])


def expert_gates(normed, router, routes, expert_ids):
    logits = dot(normed, router, ((1,), (0,)))
    named = jnp.any(routes[:, :, None] == expert_ids[None, None, :], axis=1)
    top = jnp.max(jnp.where(named, logits, -jnp.inf), axis=1, keepdims=True)
    weights = jnp.where(named, jnp.exp(logits - top), 0.0)
    return weights / jnp.sum(weights, axis=1, keepdims=True), named


def per_device(
    activations,
    cotangent,
    doc_lengths,
    routes,
    norm_gains,
    w_qkv,
    w_out,
    w_router,
    w_gate_up,
    w_down,
):
    wires = Wires()
    tok_rows, model_width = activations.shape
    layer_count = w_qkv.shape[0]
    heads_here = HEADS // CORES
    q_width = heads_here * HEAD
    qkv_width = q_width + 2 * HEAD
    ff_width = w_down.shape[2]
    expert_count = w_router.shape[2]
    chip_tokens = CORES * tok_rows
    device_count = wires.dp_count * wires.seq_count
    seq_length = min(SEQ_LEN, tok_rows * device_count)
    depth = min(-(-(WINDOW - 1) // chip_tokens), wires.chips - 1)
    core = wires.core

    def chip_index_of(first_chip, chips):
        block = first_chip + jnp.arange(chips, dtype=jnp.int32)
        order = jnp.stack([core, 1 - core]).astype(jnp.int32)
        start = block[:, None] * chip_tokens + order[None, :] * tok_rows
        return (start[:, :, None] + jnp.arange(tok_rows, dtype=jnp.int32)).reshape(-1)

    query_index = chip_index_of(wires.chip, 1)
    key_index = chip_index_of(wires.chip - depth, depth + 1)
    query_label, query_valid, position = doc_labels(query_index, doc_lengths, seq_length)
    key_label = doc_labels(key_index, doc_lengths, seq_length)[0]
    bias = jnp.where(
        keep_rule(query_index, key_index, query_label, key_label), 0.0, HIDDEN_SCORE
    ).astype(f32)
    turn = turn_tables(position)
    valid = jnp.broadcast_to(query_valid[:, None], (chip_tokens, HEAD))
    expert_ids = jnp.arange(expert_count, dtype=jnp.int32)
    my_expert = (expert_ids == wires.dp_index)[None, :]
    route_names = jnp.pad(routes.astype(bf16), ((0, 0), (0, 128 - routes.shape[1])))
    lane = jnp.arange(128, dtype=jnp.int32)[None, :]

    small_width = -(-(expert_count + 2) // 128) * 128

    def packed_weights(layer_index):
        out_rows = w_out[layer_index].T
        qkv = w_qkv[layer_index]
        small = jnp.concatenate([w_router[layer_index], norm_gains[layer_index].T], axis=1)
        small = jnp.pad(small, ((0, 0), (0, small_width - small.shape[1])))
        fronts, backs = [], []
        for c in range(CORES):
            fronts.append(
                jnp.concatenate(
                    [
                        qkv[:, c * q_width : (c + 1) * q_width],
                        qkv[:, HEADS * HEAD + c * HEAD :][:, :HEAD],
                        qkv[:, (HEADS + KV_HEADS + c) * HEAD :][:, :HEAD],
                        small,
                    ],
                    axis=1,
                )
            )
            backs.append(out_rows[:, c * q_width : (c + 1) * q_width])
        def per_chip(first, second):
            kept = jnp.where(core == 0, first, second)
            sent = jnp.where(core == 0, second, first)
            block = wires.ordered(core, kept, wires.to_core(sent), 0)
            return block.reshape(2 * kept.shape[0], kept.shape[1])

        return per_chip(*fronts), per_chip(*backs)

    def split_front(front):
        small = front[:, qkv_width:]
        return (
            small[:, expert_count : expert_count + 2].astype(f32).T,
            front[:, :qkv_width],
            small[:, :expert_count],
        )

    packed = [packed_weights(layer_index) for layer_index in range(layer_count)]
    front_width = packed[0][0].shape[1]
    first = jnp.concatenate(packed[0], axis=1)
    cut = first.shape[1] // 256 * 128
    weights = Task(wires.chip_gather(first[:, :cut], first[:, cut:]))
    gradient = Task(wires.token_gather(cotangent, slowly=True))
    phase(weights)
    phase(weights)
    phase(weights, gradient)
    held_weights = [weights.finish()]
    stream = activations.astype(f32)
    stored = []
    for layer_index in range(layer_count):
        front = held_weights[layer_index][:, :front_width]
        out_here = held_weights[layer_index][:, front_width:]
        gain_rows, qkv_here, router = split_front(front)
        gate_up_here, down_here = w_gate_up[layer_index, 0], w_down[layer_index, 0]
        more = layer_index + 1 < layer_count
        scale_one = norm_scale(stream)
        normed_own = (stream * scale_one * gain_rows[0]).astype(bf16)
        if more:
            held_weights.append(
                wires.chip_gather_whole(
                    after(jnp.concatenate(packed[layer_index + 1], axis=1), normed_own)
                )
            )
        normed_one = wires.chip_rows(normed_own)
        mixed = dot(normed_one, qkv_here, ((1,), (0,)))
        own_keys = rope_turn(mixed[:, q_width : q_width + HEAD], turn, 1.0)
        own_pair = jnp.concatenate([own_keys, mixed[:, q_width + HEAD :]], axis=1).astype(bf16)
        keys = Task(wires.key_gather(own_pair, depth))
        phase(keys)
        table = keys.finish()
        attended, queries = attend_forward(mixed, table, bias, turn, valid)
        stream_mid = stream + wires.chip_sum(dot(attended, out_here, ((1,), (1,))))
        scale_two = norm_scale(stream_mid)
        normed_two = (stream_mid * scale_two * gain_rows[1]).astype(bf16)
        sent = normed_two
        if more:
            gradient.go(sent, *gradient.marks)
        else:
            gradient.go(sent, *gradient.marks)
        if layer_index == 0:
            sent = jnp.concatenate([sent, route_names], axis=1)
        tokens = Task(wires.token_gather(sent))
        phase(tokens)
        phase(tokens)
        blocks = tokens.finish()
        if layer_index == 0:
            block_routes = [
                block[:, model_width : model_width + routes.shape[1]].astype(jnp.int32)
                for block in blocks
            ]
            blocks = [block[:, :model_width] for block in blocks]
        block_gates, up_gates, block_outs = [], [], []
        for block, route_rows in zip(blocks, block_routes):
            gates = expert_gates(block, router, route_rows, expert_ids)[0]
            gate = jnp.sum(jnp.where(my_expert, gates, 0.0), axis=1, keepdims=True)
            up_gate = dot(block, gate_up_here, ((1,), (0,)))
            hidden = jax.nn.silu(up_gate[:, :ff_width]) * up_gate[:, ff_width:] * gate
            block_gates.append(gate)
            up_gates.append(up_gate)
            block_outs.append(dot(hidden.astype(bf16), down_here, ((1,), (0,))).astype(bf16))
        stored.append(
            (
                stream,
                stream_mid,
                scale_one,
                scale_two,
                normed_one,
                normed_two,
                queries,
                table,
                attended,
                blocks,
                block_gates,
                up_gates,
                gain_rows,
                qkv_here,
                out_here,
                router,
            )
        )
        outs = Task(wires.token_scatter(block_outs))
        if more:
            phase(outs)
            phase(outs)
            stream = stream_mid + outs.finish()
    last_mid = stream_mid
    stream_grad = cotangent.astype(f32)
    grad_layers = [None] * layer_count
    held_sums = []

    def shared(value):
        rows = value.shape[0] // 2
        value = value.reshape(2, rows, value.shape[1])
        crossed = wires.to_core(place_of(value, 1 - core, 0).astype(bf16))
        return place_of(value, core, 0), crossed.astype(f32)

    for layer_index in range(layer_count - 1, -1, -1):
        (
            stream,
            stream_mid,
            scale_one,
            scale_two,
            normed_one,
            normed_two,
            queries,
            table,
            attended,
            blocks,
            block_gates,
            up_gates,
            gain_rows,
            qkv_here,
            out_here,
            router,
        ) = stored[layer_index]
        gate_up_here, down_here = w_gate_up[layer_index, 0], w_down[layer_index, 0]
        last = layer_index + 1 == layer_count
        if last:
            grad_blocks = gradient.finish()
        else:
            gradient = Task(wires.token_gather(held_grad))
            phase(gradient)
            phase(gradient)
            grad_blocks = gradient.finish()
        in_grads, pair_grads, hiddens = [], [], []
        for grad_block, gate, up_gate in zip(grad_blocks, block_gates, up_gates):
            back = dot(grad_block, down_here, ((1,), (1,)))
            gate_part = up_gate[:, :ff_width]
            up_part = up_gate[:, ff_width:]
            sigmoid_gate = jax.nn.sigmoid(gate_part)
            activated = gate_part * sigmoid_gate
            hidden = activated * up_part
            gate_grad = jnp.sum(hidden * back, axis=1, keepdims=True)
            high = gate_grad.astype(bf16).astype(f32)
            tail = jnp.where(
                lane == wires.dp_index,
                high,
                jnp.where(lane == wires.dp_index + 64, gate_grad - high, 0.0),
            ).astype(bf16)
            hidden_grad = back * gate
            pair_grad = jnp.concatenate(
                [
                    hidden_grad
                    * up_part
                    * sigmoid_gate
                    * (1.0 + gate_part * (1.0 - sigmoid_gate)),
                    hidden_grad * activated,
                ],
                axis=1,
            ).astype(bf16)
            pair_grads.append(pair_grad)
            hiddens.append((hidden * gate).astype(bf16))
            in_grad = dot(pair_grad, gate_up_here, ((1,), (1,))).astype(bf16)
            in_grads.append(jnp.concatenate([in_grad, tail], axis=1))
        earlier = [outs] if last else []
        in_grads = [after(block, *[m for task in earlier for m in task.marks]) for block in in_grads]
        back_sums = Task(wires.token_scatter(in_grads))
        phase(back_sums)
        expert_grads = Task(
            wires.expert_sums(
                [
                    (
                        jnp.concatenate(blocks, axis=0),
                        after(jnp.concatenate(pair_grads, axis=0), *in_grads),
                    ),
                    (
                        after(jnp.concatenate(hiddens, axis=0), *in_grads),
                        jnp.concatenate(grad_blocks, axis=0),
                    ),
                ]
            )
        )
        phase(back_sums, expert_grads)
        normed_grad = back_sums.finish()
        for task in earlier:
            task.go(normed_grad, *task.marks)
        gate_rows = normed_grad[:, model_width:]
        gate_rows = gate_rows[:, :expert_count] + gate_rows[:, 64 : 64 + expert_count]
        normed_grad = normed_grad[:, :model_width]
        gates, named = expert_gates(normed_two, router, routes, expert_ids)
        gate_grad = jnp.where(named, gate_rows, 0.0)
        logit_grad = gates * (gate_grad - jnp.sum(gates * gate_grad, axis=1, keepdims=True))
        logit_grad = logit_grad.astype(bf16)
        router_grad = dot(normed_two, logit_grad, ((0,), (0,)))
        normed_grad = normed_grad + dot(logit_grad, router, ((1,), (1,)))
        gain_two_grad, mid_grad = norm_back(stream_mid, scale_two, gain_rows[1], normed_grad)
        mid_grad = stream_grad + mid_grad
        attn_grad = wires.chip_rows(mid_grad.astype(bf16))
        head_grad = dot(attn_grad, out_here, ((1,), (0,))) * query_valid[:, None]
        head_grad = head_grad.astype(bf16)
        out_grad = dot(attn_grad, attended, ((0,), (0,))).astype(bf16)
        background = earlier
        if not last:
            half = q_width // 2
            out_sums = Task(wires.chip_scatter(out_grad[:, :half], out_grad[:, half:]))
            background = [out_sums]
        query_lin, key_grad, value_grad = attend_backward(queries, head_grad, table, bias, turn)
        events = [mark for task in background for mark in task.marks]
        pair_sums = after(jnp.concatenate([key_grad, value_grad], axis=1), *events)
        for task in background:
            task.go(query_lin, *events)
        key_sums = Task(wires.key_scatter(pair_sums, depth))
        phase(key_sums, *([expert_grads] if last else [out_sums]))
        own_grad = key_sums.finish()
        key_lin = rope_turn(own_grad[:, :HEAD], turn, -1.0)
        mixed_grad = jnp.concatenate(
            [query_lin, key_lin.astype(bf16), own_grad[:, HEAD:].astype(bf16)], axis=1
        )
        normed_one_grad = wires.chip_sum(dot(mixed_grad, qkv_here, ((1,), (1,))))
        gain_one_grad, front_grad = norm_back(stream, scale_one, gain_rows[0], normed_one_grad)
        stream_grad = mid_grad + front_grad
        query_lin_grad = dot(normed_one, query_lin, ((0,), (0,))).astype(bf16)
        pair_lin_grad = dot(normed_one, mixed_grad[:, q_width:], ((0,), (0,))).astype(bf16)
        small = jnp.concatenate([router_grad, jnp.stack([gain_one_grad, gain_two_grad]).T], axis=1)
        small = jnp.pad(small, ((0, 0), (0, small_width - small.shape[1]))).astype(bf16)
        if last:
            held_grad = after(stream_grad.astype(bf16), *outs.marks)
            outs.finish()
            front = jnp.concatenate([query_lin_grad, pair_lin_grad, small], axis=1)
            total = wires.chip_scatter_whole(jnp.concatenate([front, out_grad], axis=1))
            held_sums.append((layer_index, total, None, expert_grads))
        else:
            front_sums = Task(
                wires.chip_scatter(query_lin_grad, jnp.concatenate([pair_lin_grad, small], axis=1))
            )
            held_sums.append((layer_index, front_sums, out_sums, expert_grads))
    for layer_index, front_sums, out_sums, expert_grads in held_sums:
        if out_sums is None:
            front, back = front_sums[:, :front_width], front_sums[:, front_width:]
        else:
            front, back = front_sums.finish()
            front = jnp.concatenate([front, back], axis=1)
            back = jnp.concatenate(out_sums.finish(), axis=1)
        back_own, back_other = shared(back)
        front_own, front_other = shared(front)
        out_sum = wires.ordered(core, back_own, back_other, 1)
        out_sum = out_sum.reshape(out_sum.shape[0], HEADS * HEAD).T
        small_sum = (front_own + front_other)[:, qkv_width:]
        qkv_pair = wires.ordered(core, front_own[:, :qkv_width], front_other[:, :qkv_width], 1)
        rows = qkv_pair.shape[0]
        qkv_sum = jnp.concatenate(
            [
                qkv_pair[:, :, :q_width].reshape(rows, HEADS * HEAD),
                qkv_pair[:, :, q_width : q_width + HEAD].reshape(rows, KV_HEADS * HEAD),
                qkv_pair[:, :, q_width + HEAD :].reshape(rows, KV_HEADS * HEAD),
            ],
            axis=1,
        )
        gain_sum = small_sum[:, expert_count : expert_count + 2].T
        router_sum = small_sum[:, :expert_count]
        gate_up_sum, down_sum = expert_grads.finish()
        grad_layers[layer_index] = (
            gain_sum,
            qkv_sum,
            out_sum,
            router_sum,
            gate_up_sum,
            down_sum,
        )
    layer_out = (last_mid + outs.finish()).astype(bf16)
    stacked = [jnp.stack([grad_entry[member] for grad_entry in grad_layers]) for member in range(6)]
    return (
        layer_out,
        stream_grad,
        stacked[0],
        stacked[1],
        stacked[2],
        stacked[3],
        stacked[4][:, None],
        stacked[5][:, None],
    )


def solution(mesh):
    return jax.shard_map(
        per_device,
        mesh=mesh,
        in_specs=(
            P(("dp", "seq"), None),
            P(("dp", "seq"), None),
            P(),
            P(("dp", "seq"), None),
            P(None, None, ("dp", "seq")),
            P(None, ("dp", "seq"), None),
            P(None, None, ("dp", "seq")),
            P(None, ("dp", "seq"), None),
            P(None, "dp", None, None),
            P(None, "dp", None, None),
        ),
        out_specs=(
            P(("dp", "seq"), None),
            P(("dp", "seq"), None),
            P(None, None, ("dp", "seq")),
            P(None, ("dp", "seq"), None),
            P(None, None, ("dp", "seq")),
            P(None, ("dp", "seq"), None),
            P(None, "dp", "seq", None),
            P(None, "dp", "seq", None),
        ),
        check_vma=False,
    )
```

```python
import jax
import jax.numpy as jnp
from jax import lax
from jax.experimental import pallas as pl
from jax.experimental.pallas import tpu as pltpu
from jax.sharding import PartitionSpec as P

HEADS = 12
KV_HEADS = 2
HEAD = 128
WINDOW = 1024
SEQ_LEN = 8192


norm_eps = 1e-06
rope_base = 1000000.0


ALL = ("dp", "seq")
CORES = 2
LINE = 4
HIDDEN_SCORE = -1e30
KERNEL_BYTES = 24 * 2**20
f32 = jnp.float32
bf16 = jnp.bfloat16


def dot(left, right, dims):
    return lax.dot_general(left, right, (dims, ((), ())), preferred_element_type=f32)


def after(value, *events):
    total = None
    for event in events:
        if event is None:
            continue
        sample = lax.slice(event, (0,) * event.ndim, (1,) * event.ndim).reshape(1, 1)
        sample = sample.astype(f32)
        total = sample if total is None else total + sample
    if total is None:
        return value
    there = jnp.broadcast_to((total == total).reshape((1,) * value.ndim), value.shape)
    return jnp.where(there, value, jnp.zeros_like(value))


class Task:
    def __init__(self, legs):
        self.legs = legs
        self.marks = []
        self.result = None
        self.running = True
        self.go()

    def go(self, *events):
        if not self.running:
            return
        try:
            self.marks = self.legs.send(events) if self.marks else next(self.legs)
        except StopIteration as end:
            self.running = False
            self.marks = []
            self.result = end.value

    def finish(self):
        while self.running:
            self.go(*self.marks)
        return self.result


def phase(*tasks):
    events = [mark for task in tasks for mark in task.marks]
    for task in tasks:
        task.go(*events)


def place_of(stacked, index, axis):
    return lax.dynamic_index_in_dim(stacked, index, axis, keepdims=False)


class Wires:
    def __init__(self):
        self.dp_count = lax.axis_size("dp")
        self.seq_count = lax.axis_size("seq")
        self.pairs = self.seq_count // CORES
        self.length = self.dp_count // 2
        dp_index = lax.axis_index("dp")
        seq_index = lax.axis_index("seq")
        self.dp_index = dp_index
        self.line = dp_index // 2
        self.side = dp_index % 2
        self.pair = seq_index // CORES
        self.core = seq_index % CORES
        self.chip = dp_index * self.pairs + self.pair
        self.chips = self.dp_count * self.pairs
        self.by_line = self.length == LINE and self.pairs == 2

    def to_core(self, value):
        return lax.ppermute(value, "seq", [(i, i ^ 1) for i in range(self.seq_count)])

    def to_pair(self, value):
        return lax.ppermute(value, "seq", [(i, i ^ 2) for i in range(self.seq_count)])

    def to_side(self, value):
        return lax.ppermute(value, "dp", [(i, i ^ 1) for i in range(self.dp_count)])

    def along(self, value, steps):
        count = self.dp_count
        return lax.ppermute(value, "dp", [(i, (i + 2 * steps) % count) for i in range(count)])

    def chips_on(self, value, steps):
        count = self.dp_count * self.seq_count
        offset = steps * CORES
        first, last = (max(0, -offset), min(count, count - offset))
        return lax.ppermute(value, ALL, [(i, i + offset) for i in range(first, last)])

    def ordered(self, flag, own, other, axis):
        return jnp.stack(
            [jnp.where(flag == 0, own, other), jnp.where(flag == 0, other, own)], axis=axis
        )

    def token_gather(self, value, slowly=False):
        if not self.by_line:
            return [lax.all_gather(value, "dp", axis=0, tiled=True)]
        side = self.to_side(value)
        if slowly:
            events = yield [side]
            held = after(value, *events)
            one, three = self.along(held, 1), self.along(held, 3)
            events = yield [one, three]
            two = self.along(after(value, *events), 2)
            events = yield [two]
            odd = after(jnp.concatenate([one, three], axis=0), *events)
            odd_side = self.to_side(odd)
            events = yield [odd_side]
            two = after(two, *events)
        else:
            one, three = self.along(value, 1), self.along(value, 3)
            events = yield [side, one, three]
            odd = jnp.concatenate([one, three], axis=0)
            odd_side = self.to_side(odd)
            two = self.along(after(value, *events), 2)
            events = yield [odd_side, two]
            two = after(two, *[event for event in events if event is not two])
        two_side = self.to_side(two)
        events = yield [two_side]
        return [
            jnp.concatenate([value, side], axis=0),
            jnp.concatenate([odd, odd_side], axis=0),
            jnp.concatenate([two, two_side], axis=0),
        ]

    def token_scatter(self, blocks):
        if not self.by_line:
            return lax.psum_scatter(blocks[0], "dp", scatter_dimension=0, tiled=True).astype(f32)
        rows = blocks[0].shape[0] // 2
        odd = self.to_side(blocks[1][2 * rows :])
        events = yield [odd]
        odd = (blocks[1][: 2 * rows].astype(f32) + odd.astype(f32)).astype(bf16)
        one, three = self.along(odd[:rows], -1), self.along(odd[rows:], -3)
        two = self.to_side(after(blocks[2][rows:], *events))
        events = yield [one, three, two]
        two = (blocks[2][:rows].astype(f32) + two.astype(f32)).astype(bf16)
        two = self.along(after(two, *events), -2)
        side = self.to_side(after(blocks[0][rows:], *events))
        events = yield [two, side]
        total = blocks[0][:rows].astype(f32) + side.astype(f32)
        return total + one.astype(f32) + three.astype(f32) + two.astype(f32)

    def token_owner(self):
        if not self.by_line:
            return [list(range(self.dp_count))]
        place = [lax.rem(self.line - k + self.length, self.length) * 2 for k in range(LINE)]
        return [
            [place[k] + side for side in (self.side, 1 - self.side) for k in members]
            for members in ((0,), (1, 3), (2,))
        ]

    def key_gather(self, own, depth):
        earlier = [self.chips_on(own, step) for step in range(depth, 0, -1)]
        events = yield earlier
        return jnp.concatenate(earlier + [own], axis=0)

    def key_scatter(self, sums, depth):
        rows = sums.shape[0] // (depth + 1)
        earlier = [
            self.chips_on(sums[k * rows : (k + 1) * rows].astype(bf16), k - depth)
            for k in range(depth)
        ]
        events = yield earlier
        return sum(
            (value.astype(f32) for value in earlier), sums[depth * rows :]
        )

    def expert_sums(self, pairs):
        if not self.by_line:
            totals = [dot(inputs, grads, ((0,), (0,))).astype(bf16) for inputs, grads in pairs]
            return [
                lax.psum_scatter(total, "seq", scatter_dimension=0, tiled=True).astype(f32)
                for total in totals
            ]
        kept, crossed = [], []
        for inputs, grads in pairs:
            whole = dot(inputs, grads, ((0,), (0,))).astype(bf16)
            whole = whole.reshape(2, 2, whole.shape[0] // 4, -1)
            kept.append(place_of(whole, self.core, 1))
            crossed.append(self.to_core(place_of(whole, 1 - self.core, 1)))
        events = yield crossed

        def half(k, pair):
            return place_of(kept[k], pair, 0).astype(f32) + place_of(
                crossed[k], pair, 0
            ).astype(f32)

        others = [
            self.to_pair(after(half(k, 1 - self.pair).astype(bf16), *events))
            for k in range(len(pairs))
        ]
        events = yield others
        return [half(k, self.pair) + other.astype(f32) for k, other in enumerate(others)]

    def core_groups(self):
        count = self.dp_count * self.seq_count
        return [list(range(core, count, CORES)) for core in range(CORES)]

    def chip_gather_whole(self, block):
        return lax.all_gather(
            block, ALL, axis=0, tiled=True, axis_index_groups=self.core_groups()
        )

    def chip_scatter_whole(self, whole):
        return lax.psum_scatter(
            whole, ALL, scatter_dimension=0, tiled=True, axis_index_groups=self.core_groups()
        ).astype(f32)

    def chip_gather(self, one, two, slowly=False):
        rows, width = one.shape
        block = jnp.concatenate([one, two], axis=1)
        if not self.by_line:
            return self.chip_gather_whole(block)
        pieces = [block, self.along(block, 1), None, self.along(block, 3)]
        if slowly:
            events = yield [pieces[1], pieces[3]]
            pieces[2] = self.along(after(block, *events), 2)
            events = yield [pieces[2]]
        else:
            pieces[2] = self.along(block, 2)
            events = yield pieces[1:]
        lines = jnp.zeros((LINE,) + block.shape, block.dtype)
        for k, piece in enumerate(pieces):
            place = lax.rem(self.line - k + self.length, self.length)
            lines = lax.dynamic_update_slice(lines, piece[None], (place, 0, 0))
        lines = lines if not slowly else after(lines, *events)
        one, two = lines[:, :, :width], lines[:, :, width:]
        side, pair = self.to_side(one), self.to_pair(two)
        events = yield [side, pair]
        one = self.ordered(self.side, one, after(side, *events), 1)
        two = self.ordered(self.pair, two, after(pair, *events), 1)
        pair, side = self.to_pair(one), self.to_side(two)
        events = yield [pair, side]
        one = self.ordered(self.pair, one, pair, 2)
        two = self.ordered(self.side, two, side, 1)
        return jnp.concatenate(
            [part.reshape(self.chips * rows, -1) for part in (one, two)], axis=1
        )

    def chip_scatter(self, one, two, slowly=False):
        width = one.shape[1]
        rows = one.shape[0] // self.chips
        if not self.by_line:
            total = self.chip_scatter_whole(jnp.concatenate([one, two], axis=1))
            return total[:, :width], total[:, width:]

        def added(flag, stacked, axis, got, events):
            kept = place_of(stacked, flag, axis).astype(f32)
            return (kept + after(got, *events).astype(f32)).astype(bf16)

        one = one.reshape(LINE, 2, 2, rows, -1)
        two = two.reshape(LINE, 2, 2, rows, -1)
        got_one = self.to_pair(place_of(one, 1 - self.pair, 2))
        got_two = self.to_side(place_of(two, 1 - self.side, 1))
        events = yield [got_one, got_two]
        one = added(self.pair, one, 2, got_one, events)
        two = added(self.side, two, 1, got_two, events)
        got_one = self.to_side(place_of(one, 1 - self.side, 1))
        got_two = self.to_pair(place_of(two, 1 - self.pair, 1))
        events = yield [got_one, got_two]
        one = added(self.side, one, 1, got_one, events)
        two = added(self.pair, two, 1, got_two, events)
        both = jnp.concatenate([one, two], axis=2)
        pieces = [
            place_of(both, lax.rem(self.line - k + self.length, self.length), 0)
            for k in range(LINE)
        ]
        for k in (1, 3):
            pieces[k] = self.along(pieces[k], -k)
        if slowly:
            events = yield [pieces[1], pieces[3]]
            pieces[2] = self.along(after(pieces[2], *events), -2)
            events = yield [pieces[2]]
        else:
            pieces[2] = self.along(pieces[2], -2)
            events = yield pieces[1:]
        total = sum(piece.astype(f32) for piece in pieces)
        return total[:, :width], total[:, width:]

    def chip_rows(self, value):
        return jnp.concatenate([value, self.to_core(value)], axis=0)

    def chip_sum(self, value):
        rows = value.shape[0] // 2
        return value[:rows] + self.to_core(value[rows:].astype(bf16)).astype(f32)


def doc_labels(token_index, doc_lengths, seq_length):
    doc_total = doc_lengths.shape[1]
    doc_ends = jnp.cumsum(doc_lengths, axis=1)
    clamped = jnp.maximum(token_index, 0)
    seq_number = clamped // seq_length
    position = clamped % seq_length
    seq_pick = seq_number[:, None] == jnp.arange(doc_lengths.shape[0], dtype=jnp.int32)[None, :]
    token_ends = jnp.sum(jnp.where(seq_pick[:, :, None], doc_ends[None, :, :], 0), axis=1)
    doc_number = jnp.sum((position[:, None] >= token_ends).astype(jnp.int32), axis=1)
    doc_label = jnp.where(token_index >= 0, seq_number * doc_total + doc_number, -1)
    is_valid = (doc_number < doc_total - 1).astype(jnp.float32)
    return (doc_label, is_valid, position)


def turn_tables(position):
    half_width = HEAD // 2
    frequency = rope_base ** (-jnp.arange(half_width, dtype=jnp.float32) * 2.0 / HEAD)
    angles = position.astype(jnp.float32)[:, None] * frequency[None, :]
    cosine, sine = jnp.cos(angles), jnp.sin(angles)
    return (
        jnp.concatenate([cosine, cosine], axis=1),
        jnp.concatenate([-sine, sine], axis=1),
    )


def rope_turn(vectors, turn, direction):
    half_width = HEAD // 2
    swapped = jnp.concatenate([vectors[:, half_width:], vectors[:, :half_width]], axis=1)
    return vectors * turn[0] + swapped * (direction * turn[1])


def norm_scale(stream):
    return lax.rsqrt(jnp.mean(stream * stream, axis=-1, keepdims=True) + norm_eps)


def norm_back(stream, scale, gain, out_grad):
    gain_grad = jnp.sum(out_grad * stream * scale, axis=0)
    scaled_grad = out_grad * gain
    stream_grad = scale * scaled_grad - stream * scale**3 * jnp.mean(
        scaled_grad * stream, axis=-1, keepdims=True
    )
    return (gain_grad, stream_grad)


def keep_rule(query_index, key_index, query_label, key_label):
    distance = query_index[:, None] - key_index[None, :]
    same_doc = query_label[:, None] == key_label[None, :]
    return same_doc & (distance >= 0) & (distance < WINDOW)


def turned(vectors, cosine, sine):
    return vectors * cosine + pltpu.roll(vectors, HEAD // 2, 1) * sine


def score_probs(queries, keys, bias):
    scores = dot(queries, keys, ((1,), (1,))) * HEAD ** (-0.5) + bias
    weights = jnp.exp(scores - jnp.max(scores, axis=1, keepdims=True))
    return weights * (1.0 / jnp.sum(weights, axis=1, keepdims=True))


def forward_kernel(mixed, keys, values, bias, cosine, sine, valid, attended, queries):
    turned_queries = turned(mixed[...], cosine[...], sine[...]).astype(bf16)
    queries[...] = turned_queries
    prob_rows = score_probs(turned_queries, keys[...], bias[...]).astype(bf16)
    out = dot(prob_rows, values[...], ((1,), (0,)))
    attended[...] = (out * valid[...]).astype(bf16)


def attend_forward(mixed, table, bias, turn, valid):
    rows = mixed.shape[0]
    key_rows = table.shape[0]
    heads = HEADS // CORES
    per_head = pl.BlockSpec((rows, HEAD), lambda h: (0, h))
    fixed = pl.BlockSpec((rows, HEAD), lambda h: (0, 0))
    return pl.pallas_call(
        forward_kernel,
        grid=(heads,),
        in_specs=[
            per_head,
            pl.BlockSpec((key_rows, HEAD), lambda h: (0, 0)),
            pl.BlockSpec((key_rows, HEAD), lambda h: (0, 1)),
            pl.BlockSpec((rows, key_rows), lambda h: (0, 0)),
            fixed,
            fixed,
            fixed,
        ],
        out_specs=[per_head, per_head],
        out_shape=[jax.ShapeDtypeStruct((rows, heads * HEAD), bf16)] * 2,
        compiler_params=pltpu.CompilerParams(vmem_limit_bytes=KERNEL_BYTES),
        cost_estimate=pl.CostEstimate(
            flops=4 * heads * rows * key_rows * HEAD,
            bytes_accessed=4 * rows * key_rows + 8 * rows * heads * HEAD,
            transcendentals=heads * rows * key_rows,
        ),
        name="attend_forward",
    )(mixed, table, table, bias, turn[0], turn[1], valid)


def backward_kernel(
    queries, head_grad, keys, values, bias, cosine, sine, query_grad, key_grad, value_grad
):
    scale = HEAD ** (-0.5)

    @pl.when(pl.program_id(0) == 0)
    def _():
        key_grad[...] = jnp.zeros_like(key_grad)
        value_grad[...] = jnp.zeros_like(value_grad)

    prob_rows = score_probs(queries[...], keys[...], bias[...])
    prob_grad = dot(head_grad[...], values[...], ((1,), (1,)))
    row_dot = jnp.sum(prob_rows * prob_grad, axis=1, keepdims=True)
    score_grad = (prob_rows * (prob_grad - row_dot)).astype(bf16)
    grad = dot(score_grad, keys[...], ((1,), (0,))) * scale
    query_grad[...] = turned(grad, cosine[...], -sine[...]).astype(bf16)
    key_grad[...] += dot(score_grad, queries[...], ((0,), (0,))) * scale
    value_grad[...] += dot(prob_rows.astype(bf16), head_grad[...], ((0,), (0,)))


def attend_backward(queries, head_grad, table, bias, turn):
    rows = queries.shape[0]
    key_rows = table.shape[0]
    heads = HEADS // CORES
    per_head = pl.BlockSpec((rows, HEAD), lambda h: (0, h))
    fixed = pl.BlockSpec((rows, HEAD), lambda h: (0, 0))
    table_grad = pl.BlockSpec((key_rows, HEAD), lambda h: (0, 0))
    return pl.pallas_call(
        backward_kernel,
        grid=(heads,),
        in_specs=[
            per_head,
            per_head,
            pl.BlockSpec((key_rows, HEAD), lambda h: (0, 0)),
            pl.BlockSpec((key_rows, HEAD), lambda h: (0, 1)),
            pl.BlockSpec((rows, key_rows), lambda h: (0, 0)),
            fixed,
            fixed,
        ],
        out_specs=[per_head, table_grad, table_grad],
        out_shape=[
            jax.ShapeDtypeStruct((rows, heads * HEAD), bf16),
            jax.ShapeDtypeStruct((key_rows, HEAD), f32),
            jax.ShapeDtypeStruct((key_rows, HEAD), f32),
        ],
        compiler_params=pltpu.CompilerParams(vmem_limit_bytes=KERNEL_BYTES),
        cost_estimate=pl.CostEstimate(
            flops=10 * heads * rows * key_rows * HEAD,
            bytes_accessed=4 * rows * key_rows + 8 * rows * heads * HEAD,
            transcendentals=heads * rows * key_rows,
        ),
        name="attend_backward",
    )(queries, head_grad, table, table, bias, turn[0], turn[1])


def expert_gates(normed, router, routes, expert_ids):
    logits = dot(normed, router, ((1,), (0,)))
    named = jnp.any(routes[:, :, None] == expert_ids[None, None, :], axis=1)
    top = jnp.max(jnp.where(named, logits, -jnp.inf), axis=1, keepdims=True)
    weights = jnp.where(named, jnp.exp(logits - top), 0.0)
    return weights / jnp.sum(weights, axis=1, keepdims=True), named


def per_device(
    activations,
    cotangent,
    doc_lengths,
    routes,
    norm_gains,
    w_qkv,
    w_out,
    w_router,
    w_gate_up,
    w_down,
):
    wires = Wires()
    tok_rows, model_width = activations.shape
    layer_count = w_qkv.shape[0]
    heads_here = HEADS // CORES
    q_width = heads_here * HEAD
    qkv_width = q_width + 2 * HEAD
    ff_width = w_down.shape[2]
    expert_count = w_router.shape[2]
    chip_tokens = CORES * tok_rows
    device_count = wires.dp_count * wires.seq_count
    seq_length = min(SEQ_LEN, tok_rows * device_count)
    depth = min(-(-(WINDOW - 1) // chip_tokens), wires.chips - 1)
    core = wires.core

    def chip_index_of(first_chip, chips):
        block = first_chip + jnp.arange(chips, dtype=jnp.int32)
        order = jnp.stack([core, 1 - core]).astype(jnp.int32)
        start = block[:, None] * chip_tokens + order[None, :] * tok_rows
        return (start[:, :, None] + jnp.arange(tok_rows, dtype=jnp.int32)).reshape(-1)

    query_index = chip_index_of(wires.chip, 1)
    key_index = chip_index_of(wires.chip - depth, depth + 1)
    query_label, query_valid, position = doc_labels(query_index, doc_lengths, seq_length)
    key_label = doc_labels(key_index, doc_lengths, seq_length)[0]
    bias = jnp.where(
        keep_rule(query_index, key_index, query_label, key_label), 0.0, HIDDEN_SCORE
    ).astype(f32)
    turn = turn_tables(position)
    valid = jnp.broadcast_to(query_valid[:, None], (chip_tokens, HEAD))
    expert_ids = jnp.arange(expert_count, dtype=jnp.int32)
    my_expert = (expert_ids == wires.dp_index)[None, :]
    route_names = jnp.pad(routes.astype(bf16), ((0, 0), (0, 128 - routes.shape[1])))
    lane = jnp.arange(128, dtype=jnp.int32)[None, :]

    small_width = -(-(expert_count + 2) // 128) * 128

    def packed_weights(layer_index):
        out_rows = w_out[layer_index].T
        qkv = w_qkv[layer_index]
        small = jnp.concatenate([w_router[layer_index], norm_gains[layer_index].T], axis=1)
        small = jnp.pad(small, ((0, 0), (0, small_width - small.shape[1])))
        fronts, backs = [], []
        for c in range(CORES):
            fronts.append(
                jnp.concatenate(
                    [
                        qkv[:, c * q_width : (c + 1) * q_width],
                        qkv[:, HEADS * HEAD + c * HEAD :][:, :HEAD],
                        qkv[:, (HEADS + KV_HEADS + c) * HEAD :][:, :HEAD],
                        small,
                    ],
                    axis=1,
                )
            )
            backs.append(out_rows[:, c * q_width : (c + 1) * q_width])
        def per_chip(first, second):
            kept = jnp.where(core == 0, first, second)
            sent = jnp.where(core == 0, second, first)
            block = wires.ordered(core, kept, wires.to_core(sent), 0)
            return block.reshape(2 * kept.shape[0], kept.shape[1])

        return per_chip(*fronts), per_chip(*backs)

    def split_front(front):
        small = front[:, qkv_width:]
        return (
            small[:, expert_count : expert_count + 2].astype(f32).T,
            front[:, :qkv_width],
            small[:, :expert_count],
        )

    packed = [packed_weights(layer_index) for layer_index in range(layer_count)]
    front_width = packed[0][0].shape[1]
    first = jnp.concatenate(packed[0], axis=1)
    cut = first.shape[1] // 256 * 128
    weights = Task(wires.chip_gather(first[:, :cut], first[:, cut:]))
    gradient = Task(wires.token_gather(cotangent, slowly=True))
    phase(weights)
    phase(weights)
    phase(weights, gradient)
    held_weights = [weights.finish()]
    stream = activations.astype(f32)
    stored = []
    for layer_index in range(layer_count):
        front = held_weights[layer_index][:, :front_width]
        out_here = held_weights[layer_index][:, front_width:]
        gain_rows, qkv_here, router = split_front(front)
        gate_up_here, down_here = w_gate_up[layer_index, 0], w_down[layer_index, 0]
        more = layer_index + 1 < layer_count
        scale_one = norm_scale(stream)
        normed_own = (stream * scale_one * gain_rows[0]).astype(bf16)
        if more:
            held_weights.append(
                wires.chip_gather_whole(
                    after(jnp.concatenate(packed[layer_index + 1], axis=1), normed_own)
                )
            )
        normed_one = wires.chip_rows(normed_own)
        mixed = dot(normed_one, qkv_here, ((1,), (0,)))
        own_keys = rope_turn(mixed[:, q_width : q_width + HEAD], turn, 1.0)
        own_pair = jnp.concatenate([own_keys, mixed[:, q_width + HEAD :]], axis=1).astype(bf16)
        keys = Task(wires.key_gather(own_pair, depth))
        phase(keys)
        table = keys.finish()
        attended, queries = attend_forward(mixed, table, bias, turn, valid)
        stream_mid = stream + wires.chip_sum(dot(attended, out_here, ((1,), (1,))))
        scale_two = norm_scale(stream_mid)
        normed_two = (stream_mid * scale_two * gain_rows[1]).astype(bf16)
        sent = normed_two
        if more:
            gradient.go(sent, *gradient.marks)
        else:
            gradient.go(sent, *gradient.marks)
        if layer_index == 0:
            sent = jnp.concatenate([sent, route_names], axis=1)
        tokens = Task(wires.token_gather(sent))
        phase(tokens)
        phase(tokens)
        blocks = tokens.finish()
        if layer_index == 0:
            block_routes = [
                block[:, model_width : model_width + routes.shape[1]].astype(jnp.int32)
                for block in blocks
            ]
            blocks = [block[:, :model_width] for block in blocks]
        block_gates, up_gates, block_outs = [], [], []
        for block, route_rows in zip(blocks, block_routes):
            gates = expert_gates(block, router, route_rows, expert_ids)[0]
            gate = jnp.sum(jnp.where(my_expert, gates, 0.0), axis=1, keepdims=True)
            up_gate = dot(block, gate_up_here, ((1,), (0,)))
            hidden = jax.nn.silu(up_gate[:, :ff_width]) * up_gate[:, ff_width:] * gate
            block_gates.append(gate)
            up_gates.append(up_gate)
            block_outs.append(dot(hidden.astype(bf16), down_here, ((1,), (0,))).astype(bf16))
        stored.append(
            (
                stream,
                stream_mid,
                scale_one,
                scale_two,
                normed_one,
                normed_two,
                queries,
                table,
                attended,
                blocks,
                block_gates,
                up_gates,
                gain_rows,
                qkv_here,
                out_here,
                router,
            )
        )
        outs = Task(wires.token_scatter(block_outs))
        if more:
            phase(outs)
            phase(outs)
            stream = stream_mid + outs.finish()
    last_mid = stream_mid
    stream_grad = cotangent.astype(f32)
    grad_layers = [None] * layer_count
    held_sums = []

    def shared(value):
        rows = value.shape[0] // 2
        value = value.reshape(2, rows, value.shape[1])
        crossed = wires.to_core(place_of(value, 1 - core, 0).astype(bf16))
        return place_of(value, core, 0), crossed.astype(f32)

    for layer_index in range(layer_count - 1, -1, -1):
        (
            stream,
            stream_mid,
            scale_one,
            scale_two,
            normed_one,
            normed_two,
            queries,
            table,
            attended,
            blocks,
            block_gates,
            up_gates,
            gain_rows,
            qkv_here,
            out_here,
            router,
        ) = stored[layer_index]
        gate_up_here, down_here = w_gate_up[layer_index, 0], w_down[layer_index, 0]
        last = layer_index + 1 == layer_count
        if last:
            grad_blocks = gradient.finish()
        else:
            gradient = Task(wires.token_gather(held_grad))
            phase(gradient)
            phase(gradient)
            grad_blocks = gradient.finish()
        in_grads, pair_grads, hiddens = [], [], []
        for grad_block, gate, up_gate in zip(grad_blocks, block_gates, up_gates):
            back = dot(grad_block, down_here, ((1,), (1,)))
            gate_part = up_gate[:, :ff_width]
            up_part = up_gate[:, ff_width:]
            sigmoid_gate = jax.nn.sigmoid(gate_part)
            activated = gate_part * sigmoid_gate
            hidden = activated * up_part
            gate_grad = jnp.sum(hidden * back, axis=1, keepdims=True)
            high = gate_grad.astype(bf16).astype(f32)
            tail = jnp.where(
                lane == wires.dp_index,
                high,
                jnp.where(lane == wires.dp_index + 64, gate_grad - high, 0.0),
            ).astype(bf16)
            hidden_grad = back * gate
            pair_grad = jnp.concatenate(
                [
                    hidden_grad
                    * up_part
                    * sigmoid_gate
                    * (1.0 + gate_part * (1.0 - sigmoid_gate)),
                    hidden_grad * activated,
                ],
                axis=1,
            ).astype(bf16)
            pair_grads.append(pair_grad)
            hiddens.append((hidden * gate).astype(bf16))
            in_grad = dot(pair_grad, gate_up_here, ((1,), (1,))).astype(bf16)
            in_grads.append(jnp.concatenate([in_grad, tail], axis=1))
        earlier = [outs] if last else []
        in_grads = [after(block, *[m for task in earlier for m in task.marks]) for block in in_grads]
        back_sums = Task(wires.token_scatter(in_grads))
        phase(back_sums)
        expert_grads = Task(
            wires.expert_sums(
                [
                    (
                        jnp.concatenate(blocks, axis=0),
                        after(jnp.concatenate(pair_grads, axis=0), *in_grads),
                    ),
                    (
                        after(jnp.concatenate(hiddens, axis=0), *in_grads),
                        jnp.concatenate(grad_blocks, axis=0),
                    ),
                ]
            )
        )
        phase(back_sums, expert_grads)
        normed_grad = back_sums.finish()
        for task in earlier:
            task.go(normed_grad, *task.marks)
        gate_rows = normed_grad[:, model_width:]
        gate_rows = gate_rows[:, :expert_count] + gate_rows[:, 64 : 64 + expert_count]
        normed_grad = normed_grad[:, :model_width]
        gates, named = expert_gates(normed_two, router, routes, expert_ids)
        gate_grad = jnp.where(named, gate_rows, 0.0)
        logit_grad = gates * (gate_grad - jnp.sum(gates * gate_grad, axis=1, keepdims=True))
        logit_grad = logit_grad.astype(bf16)
        router_grad = dot(normed_two, logit_grad, ((0,), (0,)))
        normed_grad = normed_grad + dot(logit_grad, router, ((1,), (1,)))
        gain_two_grad, mid_grad = norm_back(stream_mid, scale_two, gain_rows[1], normed_grad)
        mid_grad = stream_grad + mid_grad
        attn_grad = wires.chip_rows(mid_grad.astype(bf16))
        head_grad = dot(attn_grad, out_here, ((1,), (0,))) * query_valid[:, None]
        head_grad = head_grad.astype(bf16)
        out_grad = dot(attn_grad, attended, ((0,), (0,))).astype(bf16)
        background = earlier
        if not last:
            half = q_width // 2
            out_sums = Task(wires.chip_scatter(out_grad[:, :half], out_grad[:, half:]))
            background = [out_sums]
        query_lin, key_grad, value_grad = attend_backward(queries, head_grad, table, bias, turn)
        events = [mark for task in background for mark in task.marks]
        pair_sums = after(jnp.concatenate([key_grad, value_grad], axis=1), *events)
        key_sums = Task(wires.key_scatter(pair_sums, depth))
        phase(key_sums, *([expert_grads] if last else []))
        own_grad = key_sums.finish()
        for task in background:
            task.go(own_grad, *events)
        key_lin = rope_turn(own_grad[:, :HEAD], turn, -1.0)
        mixed_grad = jnp.concatenate(
            [query_lin, key_lin.astype(bf16), own_grad[:, HEAD:].astype(bf16)], axis=1
        )
        normed_one_grad = wires.chip_sum(dot(mixed_grad, qkv_here, ((1,), (1,))))
        gain_one_grad, front_grad = norm_back(stream, scale_one, gain_rows[0], normed_one_grad)
        stream_grad = mid_grad + front_grad
        query_lin_grad = dot(normed_one, query_lin, ((0,), (0,))).astype(bf16)
        pair_lin_grad = dot(normed_one, mixed_grad[:, q_width:], ((0,), (0,))).astype(bf16)
        small = jnp.concatenate([router_grad, jnp.stack([gain_one_grad, gain_two_grad]).T], axis=1)
        small = jnp.pad(small, ((0, 0), (0, small_width - small.shape[1]))).astype(bf16)
        if last:
            held_grad = after(stream_grad.astype(bf16), *outs.marks)
            outs.finish()
            front = jnp.concatenate([query_lin_grad, pair_lin_grad, small], axis=1)
            total = wires.chip_scatter_whole(jnp.concatenate([front, out_grad], axis=1))
            held_sums.append((layer_index, total, None, expert_grads))
        else:
            front_sums = Task(
                wires.chip_scatter(query_lin_grad, jnp.concatenate([pair_lin_grad, small], axis=1))
            )
            held_sums.append((layer_index, front_sums, out_sums, expert_grads))
    for layer_index, front_sums, out_sums, expert_grads in held_sums:
        if out_sums is None:
            front, back = front_sums[:, :front_width], front_sums[:, front_width:]
        else:
            front, back = front_sums.finish()
            front = jnp.concatenate([front, back], axis=1)
            back = jnp.concatenate(out_sums.finish(), axis=1)
        back_own, back_other = shared(back)
        front_own, front_other = shared(front)
        out_sum = wires.ordered(core, back_own, back_other, 1)
        out_sum = out_sum.reshape(out_sum.shape[0], HEADS * HEAD).T
        small_sum = (front_own + front_other)[:, qkv_width:]
        qkv_pair = wires.ordered(core, front_own[:, :qkv_width], front_other[:, :qkv_width], 1)
        rows = qkv_pair.shape[0]
        qkv_sum = jnp.concatenate(
            [
                qkv_pair[:, :, :q_width].reshape(rows, HEADS * HEAD),
                qkv_pair[:, :, q_width : q_width + HEAD].reshape(rows, KV_HEADS * HEAD),
                qkv_pair[:, :, q_width + HEAD :].reshape(rows, KV_HEADS * HEAD),
            ],
            axis=1,
        )
        gain_sum = small_sum[:, expert_count : expert_count + 2].T
        router_sum = small_sum[:, :expert_count]
        gate_up_sum, down_sum = expert_grads.finish()
        grad_layers[layer_index] = (
            gain_sum,
            qkv_sum,
            out_sum,
            router_sum,
            gate_up_sum,
            down_sum,
        )
    layer_out = (last_mid + outs.finish()).astype(bf16)
    stacked = [jnp.stack([grad_entry[member] for grad_entry in grad_layers]) for member in range(6)]
    return (
        layer_out,
        stream_grad,
        stacked[0],
        stacked[1],
        stacked[2],
        stacked[3],
        stacked[4][:, None],
        stacked[5][:, None],
    )


def solution(mesh):
    return jax.shard_map(
        per_device,
        mesh=mesh,
        in_specs=(
            P(("dp", "seq"), None),
            P(("dp", "seq"), None),
            P(),
            P(("dp", "seq"), None),
            P(None, None, ("dp", "seq")),
            P(None, ("dp", "seq"), None),
            P(None, None, ("dp", "seq")),
            P(None, ("dp", "seq"), None),
            P(None, "dp", None, None),
            P(None, "dp", None, None),
        ),
        out_specs=(
            P(("dp", "seq"), None),
            P(("dp", "seq"), None),
            P(None, None, ("dp", "seq")),
            P(None, ("dp", "seq"), None),
            P(None, None, ("dp", "seq")),
            P(None, ("dp", "seq"), None),
            P(None, "dp", "seq", None),
            P(None, "dp", "seq", None),
        ),
        check_vma=False,
    )
```
